128 devices in a mesh: ctx: 32 (over z, x, core), col: 4 (over y).
Axes of the slice: x: 4, y: 4, z: 4, core: 2. Of those that a mesh axis runs over, the one named last changes fastest.
Arguments:
- sequence: bfloat16 [16384, 4096], P('ctx', 'col'), may hold values from -6 to 6
- w_proj: bfloat16 [4096, 3, 2048], P('col'), may hold values from -0.125 to 0.125
- short_filter: float32 [3, 3, 2048], P(None, None, 'col'), may hold values from -3 to 3
- long_filter: float32 [16384, 2048], P('ctx', 'col'), may hold values from -0.046875 to 0.046875
- skip_gain: float32 [2048], P('col'), may hold values from 0.5 to 1.5
Outputs:
- mixed: float32 [16384, 2048], P('ctx', 'col')
The draws below stay inside these ranges and needn't reach their ends.
All inputs are finite; a program needn't handle non-finite values.
Results may differ from the reference program's by a relative error of at most 0.0003.
Values sent between devices are 32-bit elements; how exact they have to be, the bound alone decides.
A program may use at most 128 MiB of HBM per device.

```python
import jax
import jax.numpy as jnp
from jax import lax

D = 4096
C = 2048
TOK_DEV = 512
TOKENS = 16384


def strengthened(drawn, own_key, source, target, shards_of, factor):
    def block_of(axis_at):
        return (jnp.arange(drawn.shape[axis_at]) // (drawn.shape[axis_at] // shards_of)).reshape((-1,) + (1,) * (drawn.ndim - 1 - axis_at))

    one_side = jax.random.permutation(own_key, shards_of)[block_of(target)]
    second = (block_of(target) + shards_of // 2) % shards_of
    return jnp.where((block_of(source) == one_side) | (block_of(source) == second), factor * drawn, drawn)


def steps_of(own_key, dims, pieces, low, largest):
    level = 1.0
    for axis_at, parts in pieces:
        steps = jax.random.uniform(jax.random.fold_in(jax.random.fold_in(own_key, 6), axis_at), (parts,), jnp.float32, low / len(pieces), largest / len(pieces))
        level = level * jnp.repeat(jnp.exp(steps), dims[axis_at] // parts).reshape((-1,) + (1,) * (len(dims) - 1 - axis_at))
    return level


def centred(own_key, dims, spread, reach, cuts=(), dtype=jnp.bfloat16):
    level = steps_of(own_key, dims, cuts, -0.22, 0.18) if cuts else 1.0
    result = jax.random.normal(own_key, dims, jnp.float32) * spread * level
    return jnp.minimum(jnp.maximum(result, -reach), reach).astype(dtype)


def heavy_noise(stream_key, dims, spread, most, pieces, heavy, held_as=jnp.bfloat16):
    result = spread * jax.random.normal(stream_key, dims, jnp.float32)
    if pieces:
        result = result * steps_of(stream_key, dims, pieces, -0.22, 0.18)
    return jnp.clip(strengthened(result, jax.random.fold_in(stream_key, 3), *heavy), -most, most).astype(held_as)


def setup_inputs(seed: int = 0) -> dict:
    keys = jax.random.split(jax.random.key(seed), 6)
    sequence = centred(keys[0], (TOKENS, D), 1.0, 6.0, ((0, 32), (1, 4)))
    w_proj = heavy_noise(keys[1], (D, 3, C), D ** -0.5, 0.125, ((0, 4),), (0, 2, 4, 2.0))
    short_filter = centred(keys[2], (3, 3, C), 0.6, 3.0, ((2, 4),), jnp.float32)
    long_filter = centred(keys[3], (TOKENS, C), TOKENS ** -0.5, 0.046875, ((0, 32), (1, 4)), jnp.float32)
    skip_gain = jnp.clip(0.5 + 1.0 * jax.random.uniform(keys[4], (C,), jnp.float32) ** steps_of(keys[4], (C,), ((0, 4),), -0.2, 0.2), 0.5, 1.5)
    return {"sequence": sequence, "w_proj": w_proj, "short_filter": short_filter, "long_filter": long_filter, "skip_gain": skip_gain}


def reference(sequence, w_proj, short_filter, long_filter, skip_gain):
    flat_weight = w_proj.reshape(D, 3 * C)
    blocks = sequence.reshape(TOKENS // TOK_DEV, TOK_DEV, D)

    def project(block):
        return jnp.dot(block, flat_weight, preferred_element_type=jnp.float32)

    projected = lax.map(project, blocks).reshape(TOKENS, 3, C)
    shaped = short_filter[0] * projected + short_filter[1] * jnp.roll(projected, 1, axis=0) + short_filter[2] * jnp.roll(projected, 2, axis=0)
    query_rows = shaped[:, 0, :]
    gated_values = shaped[:, 1, :] * shaped[:, 2, :]
    spectrum = jnp.fft.rfft(gated_values, axis=0) * jnp.fft.rfft(long_filter, axis=0)
    convolved = jnp.fft.irfft(spectrum, n=TOKENS, axis=0)
    return (query_rows * (convolved + skip_gain * gated_values)).astype(jnp.float32)
```

```python
import numpy as np

import jax
import jax.numpy as jnp
from jax import lax
from jax.sharding import PartitionSpec as P

HIGH = lax.Precision.HIGH


def tables(blocks, rows):
    total = blocks * rows
    outer = np.arange(blocks // 2 + 1)
    inner = np.arange(rows)
    fold = np.arange(blocks)
    a = 2 * np.pi / blocks * (outer[:, None] * fold[None, :] % blocks)
    t = 2 * np.pi / total * (outer[:, None] * inner[None, :] % total)
    f = 2 * np.pi / rows * (inner[:, None] * inner[None, :] % rows)
    both = np.float32
    return [(np.cos(v).astype(both), np.sin(v).astype(both)) for v in (a, t, f)]


def spectrum(x):
    (ac, asn), (tc, ts), (fc, fs) = tables(x.shape[0], x.shape[2])
    re = jnp.einsum("ks,scr->kcr", ac, x, precision=lax.Precision.HIGHEST)
    im = -jnp.einsum("ks,scr->kcr", asn, x, precision=lax.Precision.HIGHEST)
    tc, ts = tc[:, None, :], ts[:, None, :]
    re, im = re * tc + im * ts, im * tc - re * ts
    both = jnp.concatenate([re, im], axis=2)
    turn = np.block([[fc, -fs], [fs, fc]])
    out = jnp.einsum("kcr,rf->kcf", both, turn, precision=HIGH)
    return jnp.split(out, 2, axis=2)


def back(re, im, blocks):
    (ac, asn), (tc, ts), (fc, fs) = tables(blocks, re.shape[2])
    both = jnp.concatenate([re, im], axis=2)
    turn = np.block([[fc, fs], [-fs, fc]])
    re, im = jnp.split(jnp.einsum("kcr,rf->kcf", both, turn, precision=HIGH), 2, axis=2)
    tc, ts = tc[:, None, :], ts[:, None, :]
    re, im = re * tc - im * ts, im * tc + re * ts
    twice = np.full((blocks // 2 + 1, 1), 2.0, np.float32)
    twice[0] = twice[-1] = 1.0
    return jnp.einsum("ks,kcr->scr", ac * twice, re, precision=lax.Precision.HIGHEST) - jnp.einsum(
        "ks,kcr->scr", asn * twice, im, precision=lax.Precision.HIGHEST
    )


def on_device(sequence, w_proj, short_filter, long_filter, skip_gain):
    rows = sequence.shape[0]
    blocks = lax.axis_size("ctx")
    w = w_proj.transpose(1, 0, 2)
    h = lax.all_to_all(long_filter.T.reshape(blocks, -1, rows), "ctx", 0, 0, tiled=False)
    h_re, h_im = spectrum(h)
    partial = jnp.einsum("td,jdc->jtc", sequence, w, preferred_element_type=jnp.float32)
    projected = lax.psum_scatter(partial, "col", scatter_dimension=2, tiled=True)
    size = blocks
    rim = lax.ppermute(projected[:, rows - 2 :], "ctx", [((i - 1) % size, i) for i in range(size)])
    padded = jnp.concatenate([rim, projected], axis=1)
    taps = short_filter[:, :, None, :]
    shaped = taps[0] * projected + taps[1] * padded[:, 1 : rows + 1] + taps[2] * padded[:, 0:rows]
    gated = shaped[1] * shaped[2]
    u = lax.all_to_all(gated.T.reshape(blocks, -1, rows), "ctx", 0, 0, tiled=False)
    re, im = spectrum(u)
    scale = 1.0 / (blocks * rows)
    y_re, y_im = (re * h_re - im * h_im) * scale, (re * h_im + im * h_re) * scale
    y = back(y_re, y_im, blocks)
    conv = lax.all_to_all(y, "ctx", 0, 0, tiled=False).reshape(-1, rows).T
    return shaped[0] * (conv + skip_gain * gated)


def solution(mesh):
    return jax.shard_map(
        on_device,
        mesh=mesh,
        in_specs=(
            P("ctx", "col"),
            P("col", None, None),
            P(None, None, "col"),
            P("ctx", "col"),
            P("col"),
        ),
        out_specs=P("ctx", "col"),
        check_vma=False,
    )
```

```python
import functools

import ml_dtypes
import numpy as np

import jax
import jax.numpy as jnp
from jax import lax
from jax.experimental import pallas as pl
from jax.experimental.pallas import tpu as pltpu
from jax.sharding import PartitionSpec as P

MESH = pl.DeviceIdType.MESH
F32 = jnp.float32
BF16 = jnp.bfloat16
LANES = 128
RIM = 8

TILES = ((1, 0), (2, 0), (1, 1), (2, 1), (0, 0), (0, 1))


def tables(blocks, rows):
    outer, inner = np.arange(blocks // 2 + 1), np.arange(rows)
    turn = 2 * np.pi / (blocks * rows) * (outer[:, None] * inner[None, :] % (blocks * rows))
    angle = 2 * np.pi / rows * (inner[:, None] * inner[None, :] % rows)
    result = []
    for full in (np.cos(angle), np.sin(angle)):
        high = full.astype(ml_dtypes.bfloat16)
        result += [high, (full - high.astype(np.float64)).astype(ml_dtypes.bfloat16)]
    return result + [np.cos(turn).astype(np.float32), np.sin(turn).astype(np.float32)]


def scaled(value, factor):
    return value if factor == 1.0 else value * factor


def turned(value, k, n, sign):
    re, im = value
    c, s = float(np.cos(2 * np.pi * k / n)), sign * float(np.sin(2 * np.pi * k / n))
    if k == 0:
        return value
    if 4 * k == n:
        return (None if im is None else im * -s, re * s)
    if im is None:
        return (re * c, re * s)
    return (re * c - im * s, re * s + im * c)


def plus(a, b):
    return a if b is None else b if a is None else a + b


def minus(a, b):
    return a if b is None else -b if a is None else a - b


def real_dft(x):
    n = len(x)
    if n == 1:
        return [(x[0], None)]
    if n == 2:
        return [(x[0] + x[1], None), (x[0] - x[1], None)]
    even, odd = real_dft(x[0::2]), real_dft(x[1::2])
    result = [None] * (n // 2 + 1)
    for k in range(n // 4 + 1):
        (er, ei), (orr, oi) = even[k], turned(odd[k], k, n, -1.0)
        result[k] = (plus(er, orr), plus(ei, oi))
        if 2 * k != n // 2:
            result[n // 2 - k] = (minus(er, orr), minus(oi, ei) if ei is not None or oi is not None else None)
    return result


def real_inverse(f, n):
    if n == 2:
        return [f[0][0] + f[1][0], f[0][0] - f[1][0]]
    even, odd = [], []
    for k in range(n // 4 + 1):
        (ar, ai), (br, bi) = f[k], f[n // 2 - k]
        if 2 * k == n // 2:
            even.append((ar + ar, None))
            odd.append((None if ai is None else -2.0 * ai, None))
            continue
        even.append((ar + br, None if k == 0 else minus(ai, bi)))
        odd.append(turned((ar - br, None if k == 0 else plus(ai, bi)), k, n, 1.0))
    result = [None] * n
    result[0::2] = real_inverse(even, n // 2)
    result[1::2] = real_inverse(odd, n // 2)
    return result


def split(value):
    high = value.astype(BF16)
    return high, (value - high.astype(F32)).astype(BF16)


def kernel(
    blocks,
    x_ref,
    w_hbm,
    taps_ref,
    h_ref,
    gain_ref,
    table_hbm,
    turn_ref,
    out_ref,
    w_vm,
    table,
    part,
    relay,
    from_sum,
    from_one,
    fin,
    h_sent,
    h_got,
    u_kept,
    u_sent,
    u_got,
    y_sent,
    y_got,
    h_freq,
    work,
    w_sem,
    table_sem,
    tile_send,
    tile_recv,
    rim_send,
    rim_recv,
    swap_send,
    swap_recv,
):
    me, row = lax.axis_index("ctx"), lax.axis_index("col")
    rows, wide = x_ref.shape[0], part.shape[3]
    per = wide // blocks
    freqs = blocks // 2 + 1
    half = freqs * per
    tiles = len(TILES)
    peers = blocks - 1

    def at_col(offset):
        return (me, lax.rem(row + offset, 4))

    def peer(i):
        return lax.rem(me + i, blocks)

    def weight_copy(t, o):
        j, g = TILES[t]
        start = pl.multiple_of(lax.rem(row + o, 4) * (2 * wide) + g * wide, LANES)
        return pltpu.make_async_copy(w_hbm.at[j, :, pl.ds(start, wide)], w_vm.at[t, o], w_sem.at[t, o])

    barrier = pltpu.get_barrier_semaphore()

    @pl.loop(1, blocks)
    def _(i):
        pl.semaphore_signal(barrier, inc=1, device_id=(peer(i), row), device_id_type=MESH)

    for offset in (1, 3):
        pl.semaphore_signal(barrier, inc=1, device_id=at_col(offset), device_id_type=MESH)

    for pair in range(tiles // 2):
        for order in ((2, 2), (3, 1), (1, 3), (0, 0)):
            for s in range(2):
                weight_copy(2 * pair + s, order[s]).start()
    table_copy = pltpu.make_async_copy(table_hbm, table, table_sem)
    table_copy.start()

    def project(t, o):
        pltpu.make_async_copy(w_vm.at[t, o], w_vm.at[t, o], w_sem.at[t, o]).wait()
        part[t, o] = jnp.dot(x_ref[...], w_vm[t, o], preferred_element_type=F32)

    def tile_copy(t, s, kind):
        onward, backward = 1 + 2 * s, 3 - 2 * s
        place, target, offset = (
            (2, relay, onward),
            (onward, from_sum, onward),
            (backward, from_one, backward),
        )[kind]
        return pltpu.make_async_remote_copy(
            src_ref=part.at[t, place],
            dst_ref=target.at[t],
            send_sem=tile_send.at[kind, t],
            recv_sem=tile_recv.at[kind, t],
            device_id=at_col(offset),
            device_id_type=MESH,
        )

    def send_far(pair):
        @pl.loop(0, 2)
        def _(s):
            project(2 * pair + s, 2)
            tile_copy(2 * pair + s, s, 0).start()

    def send_one(pair):
        @pl.loop(0, 2)
        def _(s):
            project(2 * pair + s, 3 - 2 * s)
            tile_copy(2 * pair + s, s, 2).start()

    def project_rest(pair):
        @pl.loop(0, 2)
        def _(s):
            project(2 * pair + s, 1 + 2 * s)
            project(2 * pair + s, 0)

    def send_sum(pair):
        @pl.loop(0, 2)
        def _(s):
            t = 2 * pair + s
            tile_copy(t, s, 0).wait_recv()

            @pl.loop(0, rows // LANES)
            def _(r):
                at = pl.ds(pl.multiple_of(r * LANES, LANES), LANES)
                part[t, 1 + 2 * s, at] = part[t, 1 + 2 * s, at] + relay[t, at]

            tile_copy(t, s, 1).start()

    def rim_copy(t):
        return pltpu.make_async_remote_copy(
            src_ref=fin.at[t, pl.ds(rows, RIM)],
            dst_ref=fin.at[t, pl.ds(0, RIM)],
            send_sem=rim_send.at[t],
            recv_sem=rim_recv.at[t],
            device_id=(peer(1), row),
            device_id_type=MESH,
        )

    def finish(pair):
        @pl.loop(0, 2)
        def _(s):
            t = 2 * pair + s
            tile_copy(t, s, 2).wait_recv()
            tile_copy(t, s, 1).wait_recv()
            last = pl.ds(rows - RIM, RIM)
            fin[t, pl.ds(rows, RIM)] = part[t, 0, last] + from_sum[t, last] + from_one[t, last]
            rim_copy(t).start()

            @pl.loop(0, rows // LANES - 1)
            def _(r):
                at = pl.ds(pl.multiple_of(r * LANES, LANES), LANES)
                to = pl.ds(pl.multiple_of(r * LANES + RIM, RIM), LANES)
                fin[t, to] = part[t, 0, at] + from_sum[t, at] + from_one[t, at]

            at = pl.ds(rows - LANES, LANES - RIM)
            fin[t, pl.ds(rows - LANES + RIM, LANES - RIM)] = part[t, 0, at] + from_sum[t, at] + from_one[t, at]

        @pl.loop(0, 2)
        def _(s):
            rim_copy(2 * pair + s).wait_recv()

    def shaped(t, r):
        j, g = TILES[t]
        near = fin[t, pl.ds(pl.multiple_of(r * LANES, LANES), LANES + RIM)]
        tap = [taps_ref[i, j : j + 1, g * wide : (g + 1) * wide] for i in range(3)]
        return (
            tap[0] * near[RIM:] + tap[1] * near[RIM - 1 : RIM - 1 + LANES] + tap[2] * near[RIM - 2 : RIM - 2 + LANES]
        )

    def swap_start(which, g, source, target):
        @pl.loop(1, blocks)
        def _(i):
            p = peer(i)
            if which == 2:
                src, dst = source.at[g, p], target.at[g, pl.ds(pl.multiple_of(me * per, per), per)]
            else:
                src, dst = source.at[g, pl.ds(pl.multiple_of(p * per, per), per)], target.at[g, me]
            pltpu.make_async_remote_copy(
                src_ref=src,
                dst_ref=dst,
                send_sem=swap_send.at[which, g],
                recv_sem=swap_recv.at[which, g],
                device_id=(p, row),
                device_id_type=MESH,
            ).start()

        own = pl.ds(pl.multiple_of(me * per, per), per)
        if which == 2:
            target[g, own] = source[g, me]
        else:
            target[g, me] = source[g, own]

    def swap_wait(sem, which, g):
        held = h_got.at[0, pl.ds(0, peers)]
        pltpu.make_async_copy(held, held, sem.at[which, g]).wait()

    def times_tables(value):
        high, low = split(value)
        result = []
        for i in (0, 2):
            both = jnp.dot(jnp.concatenate([high, low], axis=0), table[i], preferred_element_type=F32)
            result.append(both[: 2 * half] + both[2 * half :] + jnp.dot(high, table[i + 1], preferred_element_type=F32))
        return result

    def spectrum(source, g):
        @pl.loop(0, rows // LANES)
        def _(r):
            at = pl.ds(pl.multiple_of(r * LANES, LANES), LANES)
            found = real_dft([source[g, s, :, at] for s in range(blocks)])
            for k, (re, im) in enumerate(found):
                c, s = turn_ref[0, k : k + 1, at], turn_ref[1, k : k + 1, at]
                work[k * per : (k + 1) * per, at] = re * c if im is None else re * c + im * s
                work[half + k * per : half + (k + 1) * per, at] = -re * s if im is None else im * c - re * s

        by_cos, by_sin = times_tables(work[...])
        return by_cos[:half] + by_sin[half:], by_cos[half:] - by_sin[:half]

    def convolve(g):
        re, im = spectrum(u_got, g)
        h_re, h_im = h_freq[g, :half], h_freq[g, half:]
        product = jnp.concatenate([re * h_re - im * h_im, re * h_im + im * h_re], axis=0)
        by_cos, by_sin = times_tables(product)
        work[:half] = by_cos[:half] - by_sin[half:]
        work[half:] = by_cos[half:] + by_sin[:half]

        @pl.loop(0, rows // LANES)
        def _(r):
            at = pl.ds(pl.multiple_of(r * LANES, LANES), LANES)
            freq = []
            for k in range(freqs):
                c, s = turn_ref[0, k : k + 1, at], turn_ref[1, k : k + 1, at]
                re, im = work[k * per : (k + 1) * per, at], work[half + k * per : half + (k + 1) * per, at]
                freq.append((re * c - im * s, None if k in (0, freqs - 1) else re * s + im * c))
            for s, value in enumerate(real_inverse(freq, blocks)):
                y_sent[g, s, :, at] = value

    def gate(g):
        for r in range(rows // LANES):
            at = slice(r * LANES, (r + 1) * LANES)
            u = shaped(2 * g, r) * shaped(2 * g + 1, r)
            u_kept[g, at] = u
            u_sent[g, :, at] = u.T
        swap_start(1, g, u_sent, u_got)

    def through(g):
        swap_wait(swap_recv, 1, g)
        convolve(g)
        swap_start(2, g, y_sent, y_got)

    pl.semaphore_wait(barrier, peers + 2)
    send_far(0)
    send_one(0)
    for g in range(2):
        for r in range(rows // LANES):
            at = slice(r * LANES, (r + 1) * LANES)
            h_sent[g, :, at] = h_ref[at, g * wide : (g + 1) * wide].T
        swap_start(0, g, h_sent, h_got)
    project_rest(0)
    send_sum(0)
    send_far(1)
    send_one(1)
    project_rest(1)
    table_copy.wait()
    scale = 1.0 / (blocks * rows)
    for g in range(2):
        swap_wait(swap_recv, 0, g)

    @pl.loop(0, 2)
    def _(g):
        re, im = spectrum(h_got, g)
        h_freq[g, :half] = re * scale
        h_freq[g, half:] = im * scale

    finish(0)
    gate(0)
    send_sum(1)
    send_far(2)
    send_one(2)
    project_rest(2)
    through(0)
    finish(1)
    gate(1)
    through(1)
    send_sum(2)
    finish(2)
    for g in range(2):
        swap_wait(swap_recv, 2, g)
        for r in range(rows // LANES):
            at = slice(r * LANES, (r + 1) * LANES)
            gain = gain_ref[:, g * wide : (g + 1) * wide]
            out_ref[at, g * wide : (g + 1) * wide] = shaped(4 + g, r) * (y_got[g, :, at].T + gain * u_kept[g, at])

    @pl.loop(0, tiles // 2)
    def _(pair):
        @pl.loop(0, 2)
        def _(s):
            t = 2 * pair + s
            rim_copy(t).wait_send()
            for kind in range(3):
                tile_copy(t, s, kind).wait_send()

    for which in range(3):
        for g in range(2):
            swap_wait(swap_send, which, g)


def on_device(blocks, sequence, w_proj, short_filter, long_filter, skip_gain):
    rows, depth = sequence.shape
    channels = long_filter.shape[1]
    wide = channels // 2
    per = wide // blocks
    freqs = blocks // 2 + 1
    tiles = len(TILES)
    *turn_tables, turn_cos, turn_sin = tables(blocks, rows)
    vmem = pl.BlockSpec(memory_space=pltpu.VMEM)
    hbm = pl.BlockSpec(memory_space=pl.ANY)
    tile = (tiles, rows, wide)
    sharded = (2, blocks, per, rows)
    flipped = (2, wide, rows)
    return pl.pallas_call(
        functools.partial(kernel, blocks),
        out_shape=jax.ShapeDtypeStruct((rows, channels), F32),
        in_specs=[vmem, hbm, vmem, vmem, vmem, hbm, vmem],
        out_specs=vmem,
        scratch_shapes=[
            pltpu.VMEM((tiles, 4, depth, wide), BF16),
            pltpu.VMEM((4, rows, rows), BF16),
            pltpu.VMEM((tiles, 4, rows, wide), F32),
            pltpu.VMEM(tile, F32),
            pltpu.VMEM(tile, F32),
            pltpu.VMEM(tile, F32),
            pltpu.VMEM((tiles, rows + RIM, wide), F32),
            pltpu.VMEM(flipped, F32),
            pltpu.VMEM(sharded, F32),
            pltpu.VMEM((2, rows, wide), F32),
            pltpu.VMEM(flipped, F32),
            pltpu.VMEM(sharded, F32),
            pltpu.VMEM(sharded, F32),
            pltpu.VMEM(flipped, F32),
            pltpu.VMEM((2, 2 * freqs * per, rows), F32),
            pltpu.VMEM((2 * freqs * per, rows), F32),
            pltpu.SemaphoreType.DMA((tiles, 4)),
            pltpu.SemaphoreType.DMA,
            pltpu.SemaphoreType.DMA((3, tiles)),
            pltpu.SemaphoreType.DMA((3, tiles)),
            pltpu.SemaphoreType.DMA((tiles,)),
            pltpu.SemaphoreType.DMA((tiles,)),
            pltpu.SemaphoreType.DMA((3, 2)),
            pltpu.SemaphoreType.DMA((3, 2)),
        ],
        compiler_params=pltpu.CompilerParams(
            collective_id=0, has_side_effects=True, vmem_limit_bytes=60 << 20
        ),
        cost_estimate=pl.CostEstimate(
            flops=2 * rows * depth * 12 * channels, bytes_accessed=16 << 20, transcendentals=0
        ),
    )(
        sequence,
        w_proj.transpose(1, 0, 2),
        short_filter,
        long_filter,
        skip_gain[None, :],
        np.stack(turn_tables),
        np.stack([turn_cos, turn_sin]),
    )


def solution(mesh):
    return jax.shard_map(
        functools.partial(on_device, mesh.shape["ctx"]),
        mesh=mesh,
        in_specs=(
            P("ctx", "col"),
            P("col", None, None),
            P(None, None, "col"),
            P("ctx", "col"),
            P("col"),
        ),
        out_specs=P("ctx", "col"),
        check_vma=False,
    )
```

```python
import functools

import ml_dtypes
import numpy as np

import jax
import jax.numpy as jnp
from jax import lax
from jax.experimental import pallas as pl
from jax.experimental.pallas import tpu as pltpu
from jax.sharding import PartitionSpec as P

MESH = pl.DeviceIdType.MESH
F32 = jnp.float32
BF16 = jnp.bfloat16
LANES = 128
RIM = 8

TILES = ((1, 0), (2, 0), (1, 1), (2, 1), (0, 0), (0, 1))


def tables(blocks, rows):
    outer, inner = np.arange(blocks // 2 + 1), np.arange(rows)
    turn = 2 * np.pi / (blocks * rows) * (outer[:, None] * inner[None, :] % (blocks * rows))
    angle = 2 * np.pi / rows * (inner[:, None] * inner[None, :] % rows)
    result = []
    for full in (np.cos(angle), np.sin(angle)):
        high = full.astype(ml_dtypes.bfloat16)
        result += [high, (full - high.astype(np.float64)).astype(ml_dtypes.bfloat16)]
    return result + [np.cos(turn).astype(np.float32), np.sin(turn).astype(np.float32)]


def scaled(value, factor):
    return value if factor == 1.0 else value * factor


def turned(value, k, n, sign):
    re, im = value
    c, s = float(np.cos(2 * np.pi * k / n)), sign * float(np.sin(2 * np.pi * k / n))
    if k == 0:
        return value
    if 4 * k == n:
        return (None if im is None else im * -s, re * s)
    if im is None:
        return (re * c, re * s)
    return (re * c - im * s, re * s + im * c)


def plus(a, b):
    return a if b is None else b if a is None else a + b


def minus(a, b):
    return a if b is None else -b if a is None else a - b


def real_dft(x):
    n = len(x)
    if n == 1:
        return [(x[0], None)]
    if n == 2:
        return [(x[0] + x[1], None), (x[0] - x[1], None)]
    even, odd = real_dft(x[0::2]), real_dft(x[1::2])
    result = [None] * (n // 2 + 1)
    for k in range(n // 4 + 1):
        (er, ei), (orr, oi) = even[k], turned(odd[k], k, n, -1.0)
        result[k] = (plus(er, orr), plus(ei, oi))
        if 2 * k != n // 2:
            result[n // 2 - k] = (minus(er, orr), minus(oi, ei) if ei is not None or oi is not None else None)
    return result


def real_inverse(f, n):
    if n == 2:
        return [f[0][0] + f[1][0], f[0][0] - f[1][0]]
    even, odd = [], []
    for k in range(n // 4 + 1):
        (ar, ai), (br, bi) = f[k], f[n // 2 - k]
        if 2 * k == n // 2:
            even.append((ar + ar, None))
            odd.append((None if ai is None else -2.0 * ai, None))
            continue
        even.append((ar + br, None if k == 0 else minus(ai, bi)))
        odd.append(turned((ar - br, None if k == 0 else plus(ai, bi)), k, n, 1.0))
    result = [None] * n
    result[0::2] = real_inverse(even, n // 2)
    result[1::2] = real_inverse(odd, n // 2)
    return result


def split(value):
    high = value.astype(BF16)
    return high, (value - high.astype(F32)).astype(BF16)


def kernel(
    blocks,
    x_hbm,
    w_hbm,
    taps_ref,
    h_hbm,
    gain_ref,
    table_hbm,
    turn_ref,
    out_hbm,
    x_ref,
    h_ref,
    out_ref,
    w_vm,
    table,
    part,
    relay,
    from_sum,
    from_one,
    fin,
    h_sent,
    h_got,
    u_kept,
    u_sent,
    u_got,
    y_sent,
    y_got,
    h_freq,
    work,
    w_sem,
    side_sem,
    out_sem,
    sum_send,
    sum_recv,
    tile_send,
    tile_recv,
    rim_send,
    rim_recv,
    swap_send,
    swap_recv,
):
    me, row = lax.axis_index("ctx"), lax.axis_index("col")
    rows, wide = x_ref.shape[0], part.shape[3]
    chunks = rows // LANES
    per = wide // blocks
    freqs = blocks // 2 + 1
    half = freqs * per
    tiles = len(TILES)
    peers = blocks - 1

    def at_col(offset):
        return (me, lax.rem(row + offset, 4))

    def peer(i):
        return lax.rem(me + i, blocks)

    def weight_copy(t, o):
        j, g = TILES[t]
        start = pl.multiple_of(lax.rem(row + o, 4) * (2 * wide) + g * wide, LANES)
        return pltpu.make_async_copy(w_hbm.at[j, :, pl.ds(start, wide)], w_vm.at[t, o], w_sem.at[t, o])

    barrier = pltpu.get_barrier_semaphore()

    @pl.loop(1, blocks)
    def _(i):
        pl.semaphore_signal(barrier, inc=1, device_id=(peer(i), row), device_id_type=MESH)

    for offset in (1, 3):
        pl.semaphore_signal(barrier, inc=1, device_id=at_col(offset), device_id_type=MESH)

    x_copy = pltpu.make_async_copy(x_hbm, x_ref, side_sem.at[0])
    h_copy = pltpu.make_async_copy(h_hbm, h_ref, side_sem.at[1])
    table_copy = pltpu.make_async_copy(table_hbm, table, side_sem.at[2])
    x_copy.start()
    for pair in range(tiles // 2):
        for order in ((2, 2), (3, 1), (1, 3), (0, 0)):
            for s in range(2):
                weight_copy(2 * pair + s, order[s]).start()
        if pair == 0:
            h_copy.start()
    table_copy.start()

    def project(t, o):
        pltpu.make_async_copy(w_vm.at[t, o], w_vm.at[t, o], w_sem.at[t, o]).wait()
        part[t, o] = jnp.dot(x_ref[...], w_vm[t, o], preferred_element_type=F32)

    def tile_copy(t, s, kind):
        onward, backward = 1 + 2 * s, 3 - 2 * s
        place, target, offset = ((2, relay, onward), (backward, from_one, backward))[kind]
        return pltpu.make_async_remote_copy(
            src_ref=part.at[t, place],
            dst_ref=target.at[t],
            send_sem=tile_send.at[kind, t],
            recv_sem=tile_recv.at[kind, t],
            device_id=at_col(offset),
            device_id_type=MESH,
        )

    def sum_copy(t, s, r):
        at = pl.ds(pl.multiple_of(r * LANES, LANES), LANES)
        return pltpu.make_async_remote_copy(
            src_ref=part.at[t, 1 + 2 * s, at],
            dst_ref=from_sum.at[t, at],
            send_sem=sum_send.at[t, r],
            recv_sem=sum_recv.at[t, r],
            device_id=at_col(1 + 2 * s),
            device_id_type=MESH,
        )

    def send_far(pair):
        @pl.loop(0, 2)
        def _(s):
            project(2 * pair + s, 2)
            if pair == 0:

                @pl.when(s == 0)
                def _():
                    pl.semaphore_wait(barrier, peers + 2)

            tile_copy(2 * pair + s, s, 0).start()

    def send_one(pair):
        @pl.loop(0, 2)
        def _(s):
            project(2 * pair + s, 3 - 2 * s)
            tile_copy(2 * pair + s, s, 1).start()

    def project_rest(pair):
        @pl.loop(0, 2)
        def _(s):
            project(2 * pair + s, 1 + 2 * s)
            project(2 * pair + s, 0)

    def send_sum(pair):
        @pl.loop(0, 2)
        def _(s):
            tile_copy(2 * pair + s, s, 0).wait_recv()

        @pl.loop(0, chunks)
        def _(i):
            r = chunks - 1 - i

            @pl.loop(0, 2)
            def _(s):
                t = 2 * pair + s
                at = pl.ds(pl.multiple_of(r * LANES, LANES), LANES)
                part[t, 1 + 2 * s, at] = part[t, 1 + 2 * s, at] + relay[t, at]
                sum_copy(t, s, r).start()

    def rim_copy(t):
        return pltpu.make_async_remote_copy(
            src_ref=fin.at[t, pl.ds(rows, RIM)],
            dst_ref=fin.at[t, pl.ds(0, RIM)],
            send_sem=rim_send.at[t],
            recv_sem=rim_recv.at[t],
            device_id=(peer(1), row),
            device_id_type=MESH,
        )

    def finish_chunk(pair, r):
        @pl.loop(0, 2)
        def _(s):
            t = 2 * pair + s
            sum_copy(t, s, r).wait_recv()
            at = pl.ds(pl.multiple_of(r * LANES, LANES), LANES)
            to = pl.ds(pl.multiple_of(r * LANES + RIM, RIM), LANES)
            fin[t, to] = part[t, 0, at] + from_sum[t, at] + from_one[t, at]

    def finish_last(pair):
        @pl.loop(0, 2)
        def _(s):
            tile_copy(2 * pair + s, s, 1).wait_recv()

        finish_chunk(pair, chunks - 1)

        @pl.loop(0, 2)
        def _(s):
            rim_copy(2 * pair + s).start()

    def finish_rim(pair):
        @pl.loop(0, 2)
        def _(s):
            rim_copy(2 * pair + s).wait_recv()

    def finish(pair):
        finish_last(pair)

        @pl.loop(1, chunks)
        def _(i):
            finish_chunk(pair, chunks - 1 - i)

        finish_rim(pair)

    def shaped(t, r):
        j, g = TILES[t]
        near = fin[t, pl.ds(pl.multiple_of(r * LANES, LANES), LANES + RIM)]
        tap = [taps_ref[i, j : j + 1, g * wide : (g + 1) * wide] for i in range(3)]
        return (
            tap[0] * near[RIM:] + tap[1] * near[RIM - 1 : RIM - 1 + LANES] + tap[2] * near[RIM - 2 : RIM - 2 + LANES]
        )

    def swap_start(which, g, source, target):
        @pl.loop(1, blocks)
        def _(i):
            p = peer(i)
            if which == 2:
                src, dst = source.at[g, p], target.at[g, pl.ds(pl.multiple_of(me * per, per), per)]
            else:
                src, dst = source.at[g, pl.ds(pl.multiple_of(p * per, per), per)], target.at[g, me]
            pltpu.make_async_remote_copy(
                src_ref=src,
                dst_ref=dst,
                send_sem=swap_send.at[which, g],
                recv_sem=swap_recv.at[which, g],
                device_id=(p, row),
                device_id_type=MESH,
            ).start()

        own = pl.ds(pl.multiple_of(me * per, per), per)
        if which == 2:
            target[g, own] = source[g, me]
        else:
            target[g, me] = source[g, own]

    def swap_wait(sem, which, g):
        held = h_got.at[0, pl.ds(0, peers)]
        pltpu.make_async_copy(held, held, sem.at[which, g]).wait()

    def times_tables(value):
        high, low = split(value)
        result = []
        for i in (0, 2):
            both = jnp.dot(jnp.concatenate([high, low], axis=0), table[i], preferred_element_type=F32)
            result.append(both[: 2 * half] + both[2 * half :] + jnp.dot(high, table[i + 1], preferred_element_type=F32))
        return result

    def spectrum(source, g):
        @pl.loop(0, chunks)
        def _(r):
            at = pl.ds(pl.multiple_of(r * LANES, LANES), LANES)
            found = real_dft([source[g, s, :, at] for s in range(blocks)])
            for k, (re, im) in enumerate(found):
                c, s = turn_ref[0, k : k + 1, at], turn_ref[1, k : k + 1, at]
                work[k * per : (k + 1) * per, at] = re * c if im is None else re * c + im * s
                work[half + k * per : half + (k + 1) * per, at] = -re * s if im is None else im * c - re * s

        by_cos, by_sin = times_tables(work[...])
        return by_cos[:half] + by_sin[half:], by_cos[half:] - by_sin[:half]

    def convolve(g):
        re, im = spectrum(u_got, g)
        h_re, h_im = h_freq[g, :half], h_freq[g, half:]
        product = jnp.concatenate([re * h_re - im * h_im, re * h_im + im * h_re], axis=0)
        by_cos, by_sin = times_tables(product)
        work[:half] = by_cos[:half] - by_sin[half:]
        work[half:] = by_cos[half:] + by_sin[:half]

        @pl.loop(0, chunks)
        def _(r):
            at = pl.ds(pl.multiple_of(r * LANES, LANES), LANES)
            freq = []
            for k in range(freqs):
                c, s = turn_ref[0, k : k + 1, at], turn_ref[1, k : k + 1, at]
                re, im = work[k * per : (k + 1) * per, at], work[half + k * per : half + (k + 1) * per, at]
                freq.append((re * c - im * s, None if k in (0, freqs - 1) else re * s + im * c))
            for s, value in enumerate(real_inverse(freq, blocks)):
                y_sent[g, s, :, at] = value

    def gate(g):
        for r in range(chunks):
            at = slice(r * LANES, (r + 1) * LANES)
            u = shaped(2 * g, r) * shaped(2 * g + 1, r)
            u_kept[g, at] = u
            u_sent[g, :, at] = u.T
        swap_start(1, g, u_sent, u_got)

    def through(g):
        swap_wait(swap_recv, 1, g)
        convolve(g)
        swap_start(2, g, y_sent, y_got)

    def result(r):
        at = pl.ds(pl.multiple_of(r * LANES, LANES), LANES)
        for g in range(2):
            out_ref[at, g * wide : (g + 1) * wide] = shaped(4 + g, r) * u_kept[g, at]
        pltpu.make_async_copy(out_ref.at[at], out_hbm.at[at], out_sem.at[r]).start()

    x_copy.wait()
    send_far(0)
    send_one(0)
    h_copy.wait()
    for g in range(2):
        for r in range(chunks):
            at = slice(r * LANES, (r + 1) * LANES)
            h_sent[g, :, at] = h_ref[at, g * wide : (g + 1) * wide].T
        swap_start(0, g, h_sent, h_got)
    project_rest(0)
    send_sum(0)
    send_far(1)
    send_one(1)
    project_rest(1)
    table_copy.wait()
    scale = 1.0 / (blocks * rows)
    for g in range(2):
        swap_wait(swap_recv, 0, g)

    @pl.loop(0, 2)
    def _(g):
        re, im = spectrum(h_got, g)
        h_freq[g, :half] = re * scale
        h_freq[g, half:] = im * scale

    finish(0)
    gate(0)
    send_sum(1)
    send_far(2)
    send_one(2)
    project_rest(2)
    through(0)
    finish(1)
    gate(1)
    send_sum(2)
    through(1)
    for g in range(2):
        swap_wait(swap_recv, 2, g)
        for r in range(chunks):
            at = slice(r * LANES, (r + 1) * LANES)
            u_kept[g, at] = y_got[g, :, at].T + gain_ref[:, g * wide : (g + 1) * wide] * u_kept[g, at]
    finish_last(2)

    @pl.loop(1, chunks)
    def _(i):
        r = chunks - 1 - i
        finish_chunk(2, r)
        result(r + 1)

    finish_rim(2)
    result(0)

    @pl.loop(0, chunks)
    def _(r):
        at = pl.ds(pl.multiple_of(r * LANES, LANES), LANES)
        pltpu.make_async_copy(out_ref.at[at], out_hbm.at[at], out_sem.at[r]).wait()

    @pl.loop(0, tiles // 2)
    def _(pair):
        @pl.loop(0, 2)
        def _(s):
            t = 2 * pair + s
            rim_copy(t).wait_send()
            for kind in range(2):
                tile_copy(t, s, kind).wait_send()

            @pl.loop(0, chunks)
            def _(r):
                sum_copy(t, s, r).wait_send()

    for which in range(3):
        for g in range(2):
            swap_wait(swap_send, which, g)


def on_device(blocks, sequence, w_proj, short_filter, long_filter, skip_gain):
    rows, depth = sequence.shape
    channels = long_filter.shape[1]
    wide = channels // 2
    per = wide // blocks
    freqs = blocks // 2 + 1
    tiles = len(TILES)
    *turn_tables, turn_cos, turn_sin = tables(blocks, rows)
    vmem = pl.BlockSpec(memory_space=pltpu.VMEM)
    hbm = pl.BlockSpec(memory_space=pl.ANY)
    tile = (tiles, rows, wide)
    sharded = (2, blocks, per, rows)
    flipped = (2, wide, rows)
    return pl.pallas_call(
        functools.partial(kernel, blocks),
        out_shape=jax.ShapeDtypeStruct((rows, channels), F32),
        in_specs=[hbm, hbm, vmem, hbm, vmem, hbm, vmem],
        out_specs=hbm,
        scratch_shapes=[
            pltpu.VMEM((rows, depth), BF16),
            pltpu.VMEM((rows, channels), F32),
            pltpu.VMEM((rows, channels), F32),
            pltpu.VMEM((tiles, 4, depth, wide), BF16),
            pltpu.VMEM((4, rows, rows), BF16),
            pltpu.VMEM((tiles, 4, rows, wide), F32),
            pltpu.VMEM(tile, F32),
            pltpu.VMEM(tile, F32),
            pltpu.VMEM(tile, F32),
            pltpu.VMEM((tiles, rows + RIM, wide), F32),
            pltpu.VMEM(flipped, F32),
            pltpu.VMEM(sharded, F32),
            pltpu.VMEM((2, rows, wide), F32),
            pltpu.VMEM(flipped, F32),
            pltpu.VMEM(sharded, F32),
            pltpu.VMEM(sharded, F32),
            pltpu.VMEM(flipped, F32),
            pltpu.VMEM((2, 2 * freqs * per, rows), F32),
            pltpu.VMEM((2 * freqs * per, rows), F32),
            pltpu.SemaphoreType.DMA((tiles, 4)),
            pltpu.SemaphoreType.DMA((3,)),
            pltpu.SemaphoreType.DMA((rows // LANES,)),
            pltpu.SemaphoreType.DMA((tiles, rows // LANES)),
            pltpu.SemaphoreType.DMA((tiles, rows // LANES)),
            pltpu.SemaphoreType.DMA((2, tiles)),
            pltpu.SemaphoreType.DMA((2, tiles)),
            pltpu.SemaphoreType.DMA((tiles,)),
            pltpu.SemaphoreType.DMA((tiles,)),
            pltpu.SemaphoreType.DMA((3, 2)),
            pltpu.SemaphoreType.DMA((3, 2)),
        ],
        compiler_params=pltpu.CompilerParams(
            collective_id=0, has_side_effects=True, vmem_limit_bytes=60 << 20
        ),
        cost_estimate=pl.CostEstimate(
            flops=2 * rows * depth * 12 * channels, bytes_accessed=16 << 20, transcendentals=0
        ),
    )(
        sequence,
        w_proj.transpose(1, 0, 2),
        short_filter,
        long_filter,
        skip_gain[None, :],
        np.stack(turn_tables),
        np.stack([turn_cos, turn_sin]),
    )


def solution(mesh):
    return jax.shard_map(
        functools.partial(on_device, mesh.shape["ctx"]),
        mesh=mesh,
        in_specs=(
            P("ctx", "col"),
            P("col", None, None),
            P(None, None, "col"),
            P("ctx", "col"),
            P("col"),
        ),
        out_specs=P("ctx", "col"),
        check_vma=False,
    )
```

```python
import functools

import ml_dtypes
import numpy as np

import jax
import jax.numpy as jnp
from jax import lax
from jax.experimental import pallas as pl
from jax.experimental.pallas import tpu as pltpu
from jax.sharding import PartitionSpec as P

MESH = pl.DeviceIdType.MESH
F32 = jnp.float32
BF16 = jnp.bfloat16
LANES = 128
RIM = 8

TILES = ((1, 0), (2, 0), (1, 1), (2, 1), (0, 0), (0, 1))


def tables(blocks, rows):
    outer, inner = np.arange(blocks // 2 + 1), np.arange(rows)
    turn = 2 * np.pi / (blocks * rows) * (outer[:, None] * inner[None, :] % (blocks * rows))
    angle = 2 * np.pi / rows * (inner[:, None] * inner[None, :] % rows)
    result = []
    for full in (np.cos(angle), np.sin(angle)):
        high = full.astype(ml_dtypes.bfloat16)
        result += [high, (full - high.astype(np.float64)).astype(ml_dtypes.bfloat16)]
    return result + [np.cos(turn).astype(np.float32), np.sin(turn).astype(np.float32)]


def scaled(value, factor):
    return value if factor == 1.0 else value * factor


def turned(value, k, n, sign):
    re, im = value
    c, s = float(np.cos(2 * np.pi * k / n)), sign * float(np.sin(2 * np.pi * k / n))
    if k == 0:
        return value
    if 4 * k == n:
        return (None if im is None else im * -s, re * s)
    if im is None:
        return (re * c, re * s)
    return (re * c - im * s, re * s + im * c)


def plus(a, b):
    return a if b is None else b if a is None else a + b


def minus(a, b):
    return a if b is None else -b if a is None else a - b


def real_dft(x):
    n = len(x)
    if n == 1:
        return [(x[0], None)]
    if n == 2:
        return [(x[0] + x[1], None), (x[0] - x[1], None)]
    even, odd = real_dft(x[0::2]), real_dft(x[1::2])
    result = [None] * (n // 2 + 1)
    for k in range(n // 4 + 1):
        (er, ei), (orr, oi) = even[k], turned(odd[k], k, n, -1.0)
        result[k] = (plus(er, orr), plus(ei, oi))
        if 2 * k != n // 2:
            result[n // 2 - k] = (minus(er, orr), minus(oi, ei) if ei is not None or oi is not None else None)
    return result


def real_inverse(f, n):
    if n == 2:
        return [f[0][0] + f[1][0], f[0][0] - f[1][0]]
    even, odd = [], []
    for k in range(n // 4 + 1):
        (ar, ai), (br, bi) = f[k], f[n // 2 - k]
        if 2 * k == n // 2:
            even.append((ar + ar, None))
            odd.append((None if ai is None else -2.0 * ai, None))
            continue
        even.append((ar + br, None if k == 0 else minus(ai, bi)))
        odd.append(turned((ar - br, None if k == 0 else plus(ai, bi)), k, n, 1.0))
    result = [None] * n
    result[0::2] = real_inverse(even, n // 2)
    result[1::2] = real_inverse(odd, n // 2)
    return result


def split(value):
    high = value.astype(BF16)
    return high, (value - high.astype(F32)).astype(BF16)


def kernel(
    blocks,
    x_hbm,
    w_hbm,
    taps_ref,
    h_hbm,
    gain_ref,
    table_hbm,
    turn_ref,
    out_hbm,
    x_ref,
    h_ref,
    out_ref,
    w_vm,
    table,
    part,
    relay,
    from_sum,
    from_one,
    fin,
    h_sent,
    h_got,
    u_kept,
    u_sent,
    u_got,
    y_sent,
    y_got,
    h_freq,
    work,
    w_sem,
    side_sem,
    out_sem,
    sum_send,
    sum_recv,
    here_sem,
    tile_send,
    tile_recv,
    rim_send,
    rim_recv,
    swap_send,
    swap_recv,
):
    me, row = lax.axis_index("ctx"), lax.axis_index("col")
    rows, wide = x_ref.shape[0], part.shape[3]
    chunks = rows // LANES
    per = wide // blocks
    freqs = blocks // 2 + 1
    half = freqs * per
    tiles = len(TILES)
    peers = blocks - 1
    levels = peers.bit_length()

    def at_col(offset):
        return (me, lax.rem(row + offset, 4))

    def peer(i):
        return lax.rem(me + i, blocks)

    def across(level):
        step = 1 << level
        return (me + step - 2 * step * lax.rem(me // step, 2), row)

    def meet(level):
        if level > 0:
            pl.semaphore_wait(here_sem.at[level - 1], 1)
        if level < levels:
            pl.semaphore_signal(here_sem.at[level], inc=1, device_id=across(level), device_id_type=MESH)

    def weight_copy(t, o):
        j, g = TILES[t]
        start = pl.multiple_of(lax.rem(row + o, 4) * (2 * wide) + g * wide, LANES)
        return pltpu.make_async_copy(w_hbm.at[j, :, pl.ds(start, wide)], w_vm.at[t, o], w_sem.at[t, o])

    barrier = pltpu.get_barrier_semaphore()

    for offset in (1, 3):
        pl.semaphore_signal(barrier, inc=1, device_id=at_col(offset), device_id_type=MESH)
    for level in range(levels):
        pl.semaphore_signal(barrier, inc=1, device_id=across(level), device_id_type=MESH)

    x_copy = pltpu.make_async_copy(x_hbm, x_ref, side_sem.at[0])
    h_copy = pltpu.make_async_copy(h_hbm, h_ref, side_sem.at[1])
    table_copy = pltpu.make_async_copy(table_hbm, table, side_sem.at[2])
    x_copy.start()
    for pair in range(tiles // 2):
        for order in ((2, 2), (3, 1), (1, 3), (0, 0)):
            for s in range(2):
                weight_copy(2 * pair + s, order[s]).start()
        if pair == 0:
            h_copy.start()
    table_copy.start()

    def project(t, o):
        pltpu.make_async_copy(w_vm.at[t, o], w_vm.at[t, o], w_sem.at[t, o]).wait()
        part[t, o] = jnp.dot(x_ref[...], w_vm[t, o], preferred_element_type=F32)

    def tile_copy(t, s, kind):
        onward, backward = 1 + 2 * s, 3 - 2 * s
        place, target, offset = ((2, relay, onward), (backward, from_one, backward))[kind]
        return pltpu.make_async_remote_copy(
            src_ref=part.at[t, place],
            dst_ref=target.at[t],
            send_sem=tile_send.at[kind, t],
            recv_sem=tile_recv.at[kind, t],
            device_id=at_col(offset),
            device_id_type=MESH,
        )

    def sum_copy(t, s, r):
        at = pl.ds(pl.multiple_of(r * LANES, LANES), LANES)
        return pltpu.make_async_remote_copy(
            src_ref=part.at[t, 1 + 2 * s, at],
            dst_ref=from_sum.at[t, at],
            send_sem=sum_send.at[t, r],
            recv_sem=sum_recv.at[t, r],
            device_id=at_col(1 + 2 * s),
            device_id_type=MESH,
        )

    def send_far(pair):
        @pl.loop(0, 2)
        def _(s):
            project(2 * pair + s, 2)
            if pair == 0:

                @pl.when(s == 0)
                def _():
                    pl.semaphore_wait(barrier, levels + 2)
                    meet(0)

            tile_copy(2 * pair + s, s, 0).start()

    def send_one(pair):
        @pl.loop(0, 2)
        def _(s):
            project(2 * pair + s, 3 - 2 * s)
            tile_copy(2 * pair + s, s, 1).start()

    def project_rest(pair):
        @pl.loop(0, 2)
        def _(s):
            project(2 * pair + s, 1 + 2 * s)
            project(2 * pair + s, 0)

    def send_sum(pair):
        @pl.loop(0, 2)
        def _(s):
            tile_copy(2 * pair + s, s, 0).wait_recv()

        @pl.loop(0, chunks)
        def _(i):
            r = chunks - 1 - i

            @pl.loop(0, 2)
            def _(s):
                t = 2 * pair + s
                at = pl.ds(pl.multiple_of(r * LANES, LANES), LANES)
                part[t, 1 + 2 * s, at] = part[t, 1 + 2 * s, at] + relay[t, at]
                sum_copy(t, s, r).start()

    def rim_copy(t):
        return pltpu.make_async_remote_copy(
            src_ref=fin.at[t, pl.ds(rows, RIM)],
            dst_ref=fin.at[t, pl.ds(0, RIM)],
            send_sem=rim_send.at[t],
            recv_sem=rim_recv.at[t],
            device_id=(peer(1), row),
            device_id_type=MESH,
        )

    def finish_chunk(pair, r):
        @pl.loop(0, 2)
        def _(s):
            t = 2 * pair + s
            sum_copy(t, s, r).wait_recv()
            at = pl.ds(pl.multiple_of(r * LANES, LANES), LANES)
            to = pl.ds(pl.multiple_of(r * LANES + RIM, RIM), LANES)
            fin[t, to] = part[t, 0, at] + from_sum[t, at] + from_one[t, at]

    def finish_last(pair):
        @pl.loop(0, 2)
        def _(s):
            tile_copy(2 * pair + s, s, 1).wait_recv()

        finish_chunk(pair, chunks - 1)

        @pl.loop(0, 2)
        def _(s):
            rim_copy(2 * pair + s).start()

    def finish_rim(pair):
        @pl.loop(0, 2)
        def _(s):
            rim_copy(2 * pair + s).wait_recv()

    def finish(pair):
        finish_last(pair)

        @pl.loop(1, chunks)
        def _(i):
            finish_chunk(pair, chunks - 1 - i)

        finish_rim(pair)

    def shaped(t, r):
        j, g = TILES[t]
        near = fin[t, pl.ds(pl.multiple_of(r * LANES, LANES), LANES + RIM)]
        tap = [taps_ref[i, j : j + 1, g * wide : (g + 1) * wide] for i in range(3)]
        return (
            tap[0] * near[RIM:] + tap[1] * near[RIM - 1 : RIM - 1 + LANES] + tap[2] * near[RIM - 2 : RIM - 2 + LANES]
        )

    def swap_start(which, g, source, target):
        @pl.loop(1, blocks)
        def _(i):
            p = peer(i)
            if which == 2:
                src, dst = source.at[g, p], target.at[g, pl.ds(pl.multiple_of(me * per, per), per)]
            else:
                src, dst = source.at[g, pl.ds(pl.multiple_of(p * per, per), per)], target.at[g, me]
            pltpu.make_async_remote_copy(
                src_ref=src,
                dst_ref=dst,
                send_sem=swap_send.at[which, g],
                recv_sem=swap_recv.at[which, g],
                device_id=(p, row),
                device_id_type=MESH,
            ).start()

        own = pl.ds(pl.multiple_of(me * per, per), per)
        if which == 2:
            target[g, own] = source[g, me]
        else:
            target[g, me] = source[g, own]

    def swap_wait(sem, which, g):
        held = h_got.at[0, pl.ds(0, peers)]
        pltpu.make_async_copy(held, held, sem.at[which, g]).wait()

    def times_tables(value):
        high, low = split(value)
        result = []
        for i in (0, 2):
            both = jnp.dot(jnp.concatenate([high, low], axis=0), table[i], preferred_element_type=F32)
            result.append(both[: 2 * half] + both[2 * half :] + jnp.dot(high, table[i + 1], preferred_element_type=F32))
        return result

    def spectrum(source, g):
        @pl.loop(0, chunks)
        def _(r):
            at = pl.ds(pl.multiple_of(r * LANES, LANES), LANES)
            found = real_dft([source[g, s, :, at] for s in range(blocks)])
            for k, (re, im) in enumerate(found):
                c, s = turn_ref[0, k : k + 1, at], turn_ref[1, k : k + 1, at]
                work[k * per : (k + 1) * per, at] = re * c if im is None else re * c + im * s
                work[half + k * per : half + (k + 1) * per, at] = -re * s if im is None else im * c - re * s

        by_cos, by_sin = times_tables(work[...])
        return by_cos[:half] + by_sin[half:], by_cos[half:] - by_sin[:half]

    def convolve(g):
        re, im = spectrum(u_got, g)
        h_re, h_im = h_freq[g, :half], h_freq[g, half:]
        product = jnp.concatenate([re * h_re - im * h_im, re * h_im + im * h_re], axis=0)
        by_cos, by_sin = times_tables(product)
        work[:half] = by_cos[:half] - by_sin[half:]
        work[half:] = by_cos[half:] + by_sin[:half]

        @pl.loop(0, chunks)
        def _(r):
            at = pl.ds(pl.multiple_of(r * LANES, LANES), LANES)
            freq = []
            for k in range(freqs):
                c, s = turn_ref[0, k : k + 1, at], turn_ref[1, k : k + 1, at]
                re, im = work[k * per : (k + 1) * per, at], work[half + k * per : half + (k + 1) * per, at]
                freq.append((re * c - im * s, None if k in (0, freqs - 1) else re * s + im * c))
            for s, value in enumerate(real_inverse(freq, blocks)):
                y_sent[g, s, :, at] = value

    def gate(g):
        for r in range(chunks):
            at = slice(r * LANES, (r + 1) * LANES)
            u = shaped(2 * g, r) * shaped(2 * g + 1, r)
            u_kept[g, at] = u
            u_sent[g, :, at] = u.T
        swap_start(1, g, u_sent, u_got)

    def through(g):
        swap_wait(swap_recv, 1, g)
        convolve(g)
        swap_start(2, g, y_sent, y_got)

    def result(r):
        at = pl.ds(pl.multiple_of(r * LANES, LANES), LANES)
        for g in range(2):
            out_ref[at, g * wide : (g + 1) * wide] = shaped(4 + g, r) * u_kept[g, at]
        pltpu.make_async_copy(out_ref.at[at], out_hbm.at[at], out_sem.at[r]).start()

    x_copy.wait()
    send_far(0)
    meet(1)
    send_one(0)
    meet(2)
    h_copy.wait()
    for g in range(2):
        for r in range(chunks):
            at = slice(r * LANES, (r + 1) * LANES)
            h_sent[g, :, at] = h_ref[at, g * wide : (g + 1) * wide].T
    meet(3)
    project_rest(0)
    meet(4)
    send_sum(0)
    meet(5)
    for g in range(2):
        swap_start(0, g, h_sent, h_got)
    send_far(1)
    send_one(1)
    project_rest(1)
    table_copy.wait()
    scale = 1.0 / (blocks * rows)
    for g in range(2):
        swap_wait(swap_recv, 0, g)

    @pl.loop(0, 2)
    def _(g):
        re, im = spectrum(h_got, g)
        h_freq[g, :half] = re * scale
        h_freq[g, half:] = im * scale

    finish(0)
    gate(0)
    send_sum(1)
    send_far(2)
    send_one(2)
    project_rest(2)
    through(0)
    finish(1)
    gate(1)
    send_sum(2)
    through(1)
    for g in range(2):
        swap_wait(swap_recv, 2, g)
        for r in range(chunks):
            at = slice(r * LANES, (r + 1) * LANES)
            u_kept[g, at] = y_got[g, :, at].T + gain_ref[:, g * wide : (g + 1) * wide] * u_kept[g, at]
    finish_last(2)

    @pl.loop(1, chunks)
    def _(i):
        r = chunks - 1 - i
        finish_chunk(2, r)
        result(r + 1)

    finish_rim(2)
    result(0)

    @pl.loop(0, chunks)
    def _(r):
        at = pl.ds(pl.multiple_of(r * LANES, LANES), LANES)
        pltpu.make_async_copy(out_ref.at[at], out_hbm.at[at], out_sem.at[r]).wait()

    @pl.loop(0, tiles // 2)
    def _(pair):
        @pl.loop(0, 2)
        def _(s):
            t = 2 * pair + s
            rim_copy(t).wait_send()
            for kind in range(2):
                tile_copy(t, s, kind).wait_send()

            @pl.loop(0, chunks)
            def _(r):
                sum_copy(t, s, r).wait_send()

    for which in range(3):
        for g in range(2):
            swap_wait(swap_send, which, g)


def on_device(blocks, sequence, w_proj, short_filter, long_filter, skip_gain):
    rows, depth = sequence.shape
    channels = long_filter.shape[1]
    wide = channels // 2
    per = wide // blocks
    freqs = blocks // 2 + 1
    tiles = len(TILES)
    *turn_tables, turn_cos, turn_sin = tables(blocks, rows)
    vmem = pl.BlockSpec(memory_space=pltpu.VMEM)
    hbm = pl.BlockSpec(memory_space=pl.ANY)
    tile = (tiles, rows, wide)
    sharded = (2, blocks, per, rows)
    flipped = (2, wide, rows)
    return pl.pallas_call(
        functools.partial(kernel, blocks),
        out_shape=jax.ShapeDtypeStruct((rows, channels), F32),
        in_specs=[hbm, hbm, vmem, hbm, vmem, hbm, vmem],
        out_specs=hbm,
        scratch_shapes=[
            pltpu.VMEM((rows, depth), BF16),
            pltpu.VMEM((rows, channels), F32),
            pltpu.VMEM((rows, channels), F32),
            pltpu.VMEM((tiles, 4, depth, wide), BF16),
            pltpu.VMEM((4, rows, rows), BF16),
            pltpu.VMEM((tiles, 4, rows, wide), F32),
            pltpu.VMEM(tile, F32),
            pltpu.VMEM(tile, F32),
            pltpu.VMEM(tile, F32),
            pltpu.VMEM((tiles, rows + RIM, wide), F32),
            pltpu.VMEM(flipped, F32),
            pltpu.VMEM(sharded, F32),
            pltpu.VMEM((2, rows, wide), F32),
            pltpu.VMEM(flipped, F32),
            pltpu.VMEM(sharded, F32),
            pltpu.VMEM(sharded, F32),
            pltpu.VMEM(flipped, F32),
            pltpu.VMEM((2, 2 * freqs * per, rows), F32),
            pltpu.VMEM((2 * freqs * per, rows), F32),
            pltpu.SemaphoreType.DMA((tiles, 4)),
            pltpu.SemaphoreType.DMA((3,)),
            pltpu.SemaphoreType.DMA((rows // LANES,)),
            pltpu.SemaphoreType.DMA((tiles, rows // LANES)),
            pltpu.SemaphoreType.DMA((tiles, rows // LANES)),
            pltpu.SemaphoreType.REGULAR((blocks.bit_length() - 1,)),
            pltpu.SemaphoreType.DMA((2, tiles)),
            pltpu.SemaphoreType.DMA((2, tiles)),
            pltpu.SemaphoreType.DMA((tiles,)),
            pltpu.SemaphoreType.DMA((tiles,)),
            pltpu.SemaphoreType.DMA((3, 2)),
            pltpu.SemaphoreType.DMA((3, 2)),
        ],
        compiler_params=pltpu.CompilerParams(
            collective_id=0, has_side_effects=True, vmem_limit_bytes=60 << 20
        ),
        cost_estimate=pl.CostEstimate(
            flops=2 * rows * depth * 12 * channels, bytes_accessed=16 << 20, transcendentals=0
        ),
    )(
        sequence,
        w_proj.transpose(1, 0, 2),
        short_filter,
        long_filter,
        skip_gain[None, :],
        np.stack(turn_tables),
        np.stack([turn_cos, turn_sin]),
    )


def solution(mesh):
    return jax.shard_map(
        functools.partial(on_device, mesh.shape["ctx"]),
        mesh=mesh,
        in_specs=(
            P("ctx", "col"),
            P("col", None, None),
            P(None, None, "col"),
            P("ctx", "col"),
            P("col"),
        ),
        out_specs=P("ctx", "col"),
        check_vma=False,
    )
```

```python
import functools

import ml_dtypes
import numpy as np

import jax
import jax.numpy as jnp
from jax import lax
from jax.experimental import pallas as pl
from jax.experimental.pallas import tpu as pltpu
from jax.sharding import PartitionSpec as P

MESH = pl.DeviceIdType.MESH
F32 = jnp.float32
BF16 = jnp.bfloat16
LANES = 128
RIM = 8

TILES = ((1, 0), (2, 0), (1, 1), (2, 1), (0, 0), (0, 1))


def tables(blocks, rows):
    outer, inner = np.arange(blocks // 2 + 1), np.arange(rows)
    turn = 2 * np.pi / (blocks * rows) * (outer[:, None] * inner[None, :] % (blocks * rows))
    angle = 2 * np.pi / rows * (inner[:, None] * inner[None, :] % rows)
    result = []
    for full in (np.cos(angle), np.sin(angle)):
        high = full.astype(ml_dtypes.bfloat16)
        result += [high, (full - high.astype(np.float64)).astype(ml_dtypes.bfloat16)]
    return result + [np.cos(turn).astype(np.float32), np.sin(turn).astype(np.float32)]


def scaled(value, factor):
    return value if factor == 1.0 else value * factor


def turned(value, k, n, sign):
    re, im = value
    c, s = float(np.cos(2 * np.pi * k / n)), sign * float(np.sin(2 * np.pi * k / n))
    if k == 0:
        return value
    if 4 * k == n:
        return (None if im is None else im * -s, re * s)
    if im is None:
        return (re * c, re * s)
    return (re * c - im * s, re * s + im * c)


def plus(a, b):
    return a if b is None else b if a is None else a + b


def minus(a, b):
    return a if b is None else -b if a is None else a - b


def real_dft(x):
    n = len(x)
    if n == 1:
        return [(x[0], None)]
    if n == 2:
        return [(x[0] + x[1], None), (x[0] - x[1], None)]
    even, odd = real_dft(x[0::2]), real_dft(x[1::2])
    result = [None] * (n // 2 + 1)
    for k in range(n // 4 + 1):
        (er, ei), (orr, oi) = even[k], turned(odd[k], k, n, -1.0)
        result[k] = (plus(er, orr), plus(ei, oi))
        if 2 * k != n // 2:
            result[n // 2 - k] = (minus(er, orr), minus(oi, ei) if ei is not None or oi is not None else None)
    return result


def real_inverse(f, n):
    if n == 2:
        return [f[0][0] + f[1][0], f[0][0] - f[1][0]]
    even, odd = [], []
    for k in range(n // 4 + 1):
        (ar, ai), (br, bi) = f[k], f[n // 2 - k]
        if 2 * k == n // 2:
            even.append((ar + ar, None))
            odd.append((None if ai is None else -2.0 * ai, None))
            continue
        even.append((ar + br, None if k == 0 else minus(ai, bi)))
        odd.append(turned((ar - br, None if k == 0 else plus(ai, bi)), k, n, 1.0))
    result = [None] * n
    result[0::2] = real_inverse(even, n // 2)
    result[1::2] = real_inverse(odd, n // 2)
    return result


def split(value):
    high = value.astype(BF16)
    return high, (value - high.astype(F32)).astype(BF16)


def kernel(
    blocks,
    x_hbm,
    w_hbm,
    taps_hbm,
    h_hbm,
    gain_hbm,
    table_hbm,
    turn_hbm,
    out_ref,
    x_ref,
    taps_ref,
    h_ref,
    gain_ref,
    turn_ref,
    w_vm,
    table,
    part,
    relay,
    from_sum,
    from_one,
    fin,
    h_sent,
    h_got,
    u_kept,
    u_sent,
    u_got,
    y_sent,
    y_got,
    h_freq,
    work,
    w_sem,
    side_sem,
    far_send,
    far_recv,
    sum_send,
    sum_recv,
    here_sem,
    tile_send,
    tile_recv,
    rim_send,
    rim_recv,
    swap_send,
    swap_recv,
):
    me, row = lax.axis_index("ctx"), lax.axis_index("col")
    rows, wide = x_ref.shape[0], part.shape[3]
    chunks = rows // LANES
    per = wide // blocks
    freqs = blocks // 2 + 1
    half = freqs * per
    tiles = len(TILES)
    peers = blocks - 1
    levels = peers.bit_length()

    def at_col(offset):
        return (me, lax.rem(row + offset, 4))

    def peer(i):
        return lax.rem(me + i, blocks)

    def across(level):
        step = 1 << level
        return (me + step - 2 * step * lax.rem(me // step, 2), row)

    def meet(level):
        if level > 0:
            pl.semaphore_wait(here_sem.at[level - 1], 1)
        if level < levels:
            pl.semaphore_signal(here_sem.at[level], inc=1, device_id=across(level), device_id_type=MESH)

    def weight_copy(t, o):
        j, g = TILES[t]
        start = pl.multiple_of(lax.rem(row + o, 4) * (2 * wide) + g * wide, LANES)
        return pltpu.make_async_copy(w_hbm.at[j, :, pl.ds(start, wide)], w_vm.at[t, o], w_sem.at[t, o])

    operands = ((x_hbm, x_ref), (h_hbm, h_ref), (taps_hbm, taps_ref), (table_hbm, table), (turn_hbm, turn_ref), (gain_hbm, gain_ref))
    x_copy, h_copy, *side_copies = [
        pltpu.make_async_copy(src, dst, side_sem.at[i]) for i, (src, dst) in enumerate(operands)
    ]
    x_copy.start()
    weight_copy(0, 2).start()
    weight_copy(1, 2).start()
    barrier = pltpu.get_barrier_semaphore()
    for offset in (1, 3):
        pl.semaphore_signal(barrier, inc=1, device_id=at_col(offset), device_id_type=MESH)
    for level in range(levels):
        pl.semaphore_signal(barrier, inc=1, device_id=across(level), device_id_type=MESH)
    weight_copy(0, 3).start()
    weight_copy(1, 1).start()

    def fetch(pair):
        for order in ((2, 2), (3, 1), (1, 3), (0, 0)):
            for s in range(2):
                if pair > 0 or order[0] < 2:
                    weight_copy(2 * pair + s, order[s]).start()

    def project(t, o):
        pltpu.make_async_copy(w_vm.at[t, o], w_vm.at[t, o], w_sem.at[t, o]).wait()
        part[t, o] = jnp.dot(x_ref[...], w_vm[t, o], preferred_element_type=F32)

    def tile_copy(t, s, kind):
        onward, backward = 1 + 2 * s, 3 - 2 * s
        place, target, offset = ((2, relay, onward), (backward, from_one, backward))[kind]
        return pltpu.make_async_remote_copy(
            src_ref=part.at[t, place],
            dst_ref=target.at[t],
            send_sem=tile_send.at[kind, t],
            recv_sem=tile_recv.at[kind, t],
            device_id=at_col(offset),
            device_id_type=MESH,
        )

    def sum_copy(t, s, r):
        at = pl.ds(pl.multiple_of(r * LANES, LANES), LANES)
        return pltpu.make_async_remote_copy(
            src_ref=part.at[t, 1 + 2 * s, at],
            dst_ref=from_sum.at[t, at],
            send_sem=sum_send.at[t, r],
            recv_sem=sum_recv.at[t, r],
            device_id=at_col(1 + 2 * s),
            device_id_type=MESH,
        )

    def far_copy(t, s, r):
        at = pl.ds(pl.multiple_of(r * LANES, LANES), LANES)
        return pltpu.make_async_remote_copy(
            src_ref=part.at[t, 2, at],
            dst_ref=relay.at[t, at],
            send_sem=far_send.at[t, r],
            recv_sem=far_recv.at[t, r],
            device_id=at_col(1 + 2 * s),
            device_id_type=MESH,
        )

    def send_first():
        for s in range(2):
            pltpu.make_async_copy(w_vm.at[s, 2], w_vm.at[s, 2], w_sem.at[s, 2]).wait()

        @pl.loop(0, 2 * chunks)
        def _(i):
            r, s = i // 2, lax.rem(i, 2)
            at = pl.ds(pl.multiple_of(r * LANES, LANES), LANES)
            part[s, 2, at] = jnp.dot(x_ref[at, :], w_vm[s, 2], preferred_element_type=F32)

            @pl.when(i == 0)
            def _():
                pl.semaphore_wait(barrier, levels + 2)
                meet(0)

            far_copy(s, s, r).start()

    def send_far(pair):
        @pl.loop(0, 2)
        def _(s):
            project(2 * pair + s, 2)
            tile_copy(2 * pair + s, s, 0).start()

    def send_one(pair):
        @pl.loop(0, 2)
        def _(s):
            project(2 * pair + s, 3 - 2 * s)
            tile_copy(2 * pair + s, s, 1).start()

    def project_rest(pair):
        @pl.loop(0, 2)
        def _(s):
            project(2 * pair + s, 1 + 2 * s)
            project(2 * pair + s, 0)

    def send_sum(pair):
        if pair > 0:

            @pl.loop(0, 2)
            def _(s):
                tile_copy(2 * pair + s, s, 0).wait_recv()

        else:

            @pl.loop(0, chunks)
            def _(r):
                for s in range(2):
                    far_copy(s, s, r).wait_recv()

        @pl.loop(0, chunks)
        def _(i):
            r = chunks - 1 - i

            @pl.loop(0, 2)
            def _(s):
                t = 2 * pair + s
                at = pl.ds(pl.multiple_of(r * LANES, LANES), LANES)
                part[t, 1 + 2 * s, at] = part[t, 1 + 2 * s, at] + relay[t, at]
                sum_copy(t, s, r).start()

    def rim_copy(t):
        return pltpu.make_async_remote_copy(
            src_ref=fin.at[t, pl.ds(rows, RIM)],
            dst_ref=fin.at[t, pl.ds(0, RIM)],
            send_sem=rim_send.at[t],
            recv_sem=rim_recv.at[t],
            device_id=(peer(1), row),
            device_id_type=MESH,
        )

    def finish_chunk(pair, r):
        @pl.loop(0, 2)
        def _(s):
            t = 2 * pair + s
            sum_copy(t, s, r).wait_recv()
            at = pl.ds(pl.multiple_of(r * LANES, LANES), LANES)
            to = pl.ds(pl.multiple_of(r * LANES + RIM, RIM), LANES)
            fin[t, to] = part[t, 0, at] + from_sum[t, at] + from_one[t, at]

    def finish_last(pair):
        @pl.loop(0, 2)
        def _(s):
            tile_copy(2 * pair + s, s, 1).wait_recv()

        finish_chunk(pair, chunks - 1)

        @pl.loop(0, 2)
        def _(s):
            rim_copy(2 * pair + s).start()

    def finish_rim(pair):
        @pl.loop(0, 2)
        def _(s):
            rim_copy(2 * pair + s).wait_recv()

    def finish(pair):
        finish_last(pair)

        @pl.loop(1, chunks)
        def _(i):
            finish_chunk(pair, chunks - 1 - i)

        finish_rim(pair)

    def shaped(t, r):
        j, g = TILES[t]
        near = fin[t, pl.ds(pl.multiple_of(r * LANES, LANES), LANES + RIM)]
        tap = [taps_ref[i, j : j + 1, g * wide : (g + 1) * wide] for i in range(3)]
        return (
            tap[0] * near[RIM:] + tap[1] * near[RIM - 1 : RIM - 1 + LANES] + tap[2] * near[RIM - 2 : RIM - 2 + LANES]
        )

    def swap_start(which, g, source, target):
        @pl.loop(1, blocks)
        def _(i):
            p = peer(i)
            if which == 2:
                src, dst = source.at[g, p], target.at[g, pl.ds(pl.multiple_of(me * per, per), per)]
            else:
                src, dst = source.at[g, pl.ds(pl.multiple_of(p * per, per), per)], target.at[g, me]
            pltpu.make_async_remote_copy(
                src_ref=src,
                dst_ref=dst,
                send_sem=swap_send.at[which, g],
                recv_sem=swap_recv.at[which, g],
                device_id=(p, row),
                device_id_type=MESH,
            ).start()

        own = pl.ds(pl.multiple_of(me * per, per), per)
        if which == 2:
            target[g, own] = source[g, me]
        else:
            target[g, me] = source[g, own]

    def swap_wait(sem, which, g):
        held = h_got.at[0, pl.ds(0, peers)]
        pltpu.make_async_copy(held, held, sem.at[which, g]).wait()

    def times_tables(value):
        high, low = split(value)
        result = []
        for i in (0, 2):
            both = jnp.dot(jnp.concatenate([high, low], axis=0), table[i], preferred_element_type=F32)
            result.append(both[: 2 * half] + both[2 * half :] + jnp.dot(high, table[i + 1], preferred_element_type=F32))
        return result

    def spectrum(source, g):
        @pl.loop(0, chunks)
        def _(r):
            at = pl.ds(pl.multiple_of(r * LANES, LANES), LANES)
            found = real_dft([source[g, s, :, at] for s in range(blocks)])
            for k, (re, im) in enumerate(found):
                c, s = turn_ref[0, k : k + 1, at], turn_ref[1, k : k + 1, at]
                work[k * per : (k + 1) * per, at] = re * c if im is None else re * c + im * s
                work[half + k * per : half + (k + 1) * per, at] = -re * s if im is None else im * c - re * s

        by_cos, by_sin = times_tables(work[...])
        return by_cos[:half] + by_sin[half:], by_cos[half:] - by_sin[:half]

    def convolve(g):
        re, im = spectrum(u_got, g)
        h_re, h_im = h_freq[g, :half], h_freq[g, half:]
        product = jnp.concatenate([re * h_re - im * h_im, re * h_im + im * h_re], axis=0)
        by_cos, by_sin = times_tables(product)
        work[:half] = by_cos[:half] - by_sin[half:]
        work[half:] = by_cos[half:] + by_sin[:half]

        @pl.loop(0, chunks)
        def _(r):
            at = pl.ds(pl.multiple_of(r * LANES, LANES), LANES)
            freq = []
            for k in range(freqs):
                c, s = turn_ref[0, k : k + 1, at], turn_ref[1, k : k + 1, at]
                re, im = work[k * per : (k + 1) * per, at], work[half + k * per : half + (k + 1) * per, at]
                freq.append((re * c - im * s, None if k in (0, freqs - 1) else re * s + im * c))
            for s, value in enumerate(real_inverse(freq, blocks)):
                y_sent[g, s, :, at] = value

    def gate(g):
        for r in range(chunks):
            at = slice(r * LANES, (r + 1) * LANES)
            u = shaped(2 * g, r) * shaped(2 * g + 1, r)
            u_kept[g, at] = u
            u_sent[g, :, at] = u.T
        swap_start(1, g, u_sent, u_got)

    def through(g):
        swap_wait(swap_recv, 1, g)
        convolve(g)
        swap_start(2, g, y_sent, y_got)

    def result(r):
        at = pl.ds(pl.multiple_of(r * LANES, LANES), LANES)
        for g in range(2):
            out_ref[at, g * wide : (g + 1) * wide] = shaped(4 + g, r) * u_kept[g, at]

    x_copy.wait()
    send_first()
    meet(1)
    send_one(0)
    h_copy.start()
    fetch(0)
    meet(2)
    fetch(1)
    h_copy.wait()
    for g in range(2):
        for r in range(chunks):
            at = slice(r * LANES, (r + 1) * LANES)
            h_sent[g, :, at] = h_ref[at, g * wide : (g + 1) * wide].T
    meet(3)
    project_rest(0)
    meet(4)
    for copy in side_copies:
        copy.start()
    send_sum(0)
    meet(5)
    for g in range(2):
        swap_start(0, g, h_sent, h_got)
    fetch(2)
    send_far(1)
    send_one(1)
    project_rest(1)
    for copy in side_copies:
        copy.wait()
    scale = 1.0 / (blocks * rows)
    for g in range(2):
        swap_wait(swap_recv, 0, g)

    @pl.loop(0, 2)
    def _(g):
        re, im = spectrum(h_got, g)
        h_freq[g, :half] = re * scale
        h_freq[g, half:] = im * scale

    finish(0)
    gate(0)
    send_sum(1)
    send_far(2)
    send_one(2)
    project_rest(2)
    through(0)
    finish(1)
    gate(1)
    send_sum(2)
    through(1)
    for g in range(2):
        swap_wait(swap_recv, 2, g)
        for r in range(chunks):
            at = slice(r * LANES, (r + 1) * LANES)
            u_kept[g, at] = y_got[g, :, at].T + gain_ref[:, g * wide : (g + 1) * wide] * u_kept[g, at]
    finish_last(2)

    @pl.loop(1, chunks)
    def _(i):
        r = chunks - 1 - i
        finish_chunk(2, r)
        result(r + 1)

    finish_rim(2)
    result(0)

    @pl.loop(0, chunks)
    def _(r):
        for s in range(2):
            far_copy(s, s, r).wait_send()

    @pl.loop(0, tiles // 2)
    def _(pair):
        @pl.loop(0, 2)
        def _(s):
            t = 2 * pair + s
            rim_copy(t).wait_send()
            tile_copy(t, s, 1).wait_send()

            @pl.when(pair > 0)
            def _():
                tile_copy(t, s, 0).wait_send()

            @pl.loop(0, chunks)
            def _(r):
                sum_copy(t, s, r).wait_send()

    for which in range(3):
        for g in range(2):
            swap_wait(swap_send, which, g)


def on_device(blocks, sequence, w_proj, short_filter, long_filter, skip_gain):
    rows, depth = sequence.shape
    channels = long_filter.shape[1]
    wide = channels // 2
    per = wide // blocks
    freqs = blocks // 2 + 1
    tiles = len(TILES)
    *turn_tables, turn_cos, turn_sin = tables(blocks, rows)
    vmem = pl.BlockSpec(memory_space=pltpu.VMEM)
    hbm = pl.BlockSpec(memory_space=pl.ANY)
    tile = (tiles, rows, wide)
    sharded = (2, blocks, per, rows)
    flipped = (2, wide, rows)
    return pl.pallas_call(
        functools.partial(kernel, blocks),
        out_shape=pltpu.VMEM((rows, channels), F32),
        in_specs=[hbm] * 7,
        out_specs=vmem,
        scratch_shapes=[
            pltpu.VMEM((rows, depth), BF16),
            pltpu.VMEM(short_filter.shape, F32),
            pltpu.VMEM((rows, channels), F32),
            pltpu.VMEM((1, channels), F32),
            pltpu.VMEM((2, freqs, rows), F32),
            pltpu.VMEM((tiles, 4, depth, wide), BF16),
            pltpu.VMEM((4, rows, rows), BF16),
            pltpu.VMEM((tiles, 4, rows, wide), F32),
            pltpu.VMEM(tile, F32),
            pltpu.VMEM(tile, F32),
            pltpu.VMEM(tile, F32),
            pltpu.VMEM((tiles, rows + RIM, wide), F32),
            pltpu.VMEM(flipped, F32),
            pltpu.VMEM(sharded, F32),
            pltpu.VMEM((2, rows, wide), F32),
            pltpu.VMEM(flipped, F32),
            pltpu.VMEM(sharded, F32),
            pltpu.VMEM(sharded, F32),
            pltpu.VMEM(flipped, F32),
            pltpu.VMEM((2, 2 * freqs * per, rows), F32),
            pltpu.VMEM((2 * freqs * per, rows), F32),
            pltpu.SemaphoreType.DMA((tiles, 4)),
            pltpu.SemaphoreType.DMA((6,)),
            pltpu.SemaphoreType.DMA((2, rows // LANES)),
            pltpu.SemaphoreType.DMA((2, rows // LANES)),
            pltpu.SemaphoreType.DMA((tiles, rows // LANES)),
            pltpu.SemaphoreType.DMA((tiles, rows // LANES)),
            pltpu.SemaphoreType.REGULAR((blocks.bit_length() - 1,)),
            pltpu.SemaphoreType.DMA((2, tiles)),
            pltpu.SemaphoreType.DMA((2, tiles)),
            pltpu.SemaphoreType.DMA((tiles,)),
            pltpu.SemaphoreType.DMA((tiles,)),
            pltpu.SemaphoreType.DMA((3, 2)),
            pltpu.SemaphoreType.DMA((3, 2)),
        ],
        compiler_params=pltpu.CompilerParams(
            collective_id=0, has_side_effects=True, vmem_limit_bytes=56 << 20
        ),
        cost_estimate=pl.CostEstimate(
            flops=2 * rows * depth * 12 * channels, bytes_accessed=16 << 20, transcendentals=0
        ),
    )(
        sequence,
        w_proj.transpose(1, 0, 2),
        short_filter,
        long_filter,
        skip_gain[None, :],
        np.stack(turn_tables),
        np.stack([turn_cos, turn_sin]),
    )


def solution(mesh):
    return jax.shard_map(
        functools.partial(on_device, mesh.shape["ctx"]),
        mesh=mesh,
        in_specs=(
            P("ctx", "col"),
            P("col", None, None),
            P(None, None, "col"),
            P("ctx", "col"),
            P("col"),
        ),
        out_specs=P("ctx", "col"),
        check_vma=False,
    )
```

```python
import functools

import ml_dtypes
import numpy as np

import jax
import jax.numpy as jnp
from jax import lax
from jax.experimental import pallas as pl
from jax.experimental.pallas import tpu as pltpu
from jax.sharding import PartitionSpec as P

MESH = pl.DeviceIdType.MESH
F32 = jnp.float32
BF16 = jnp.bfloat16
LANES = 128
RIM = 8

TILES = ((1, 0), (2, 0), (1, 1), (2, 1), (0, 0), (0, 1))


def tables(blocks, rows):
    outer, inner = np.arange(blocks // 2 + 1), np.arange(rows)
    turn = 2 * np.pi / (blocks * rows) * (outer[:, None] * inner[None, :] % (blocks * rows))
    angle = 2 * np.pi / rows * (inner[:, None] * inner[None, :] % rows)
    result = []
    for full in (np.cos(angle), np.sin(angle)):
        high = full.astype(ml_dtypes.bfloat16)
        result += [high, (full - high.astype(np.float64)).astype(ml_dtypes.bfloat16)]
    return result + [np.cos(turn).astype(np.float32), np.sin(turn).astype(np.float32)]


def scaled(value, factor):
    return value if factor == 1.0 else value * factor


def turned(value, k, n, sign):
    re, im = value
    c, s = float(np.cos(2 * np.pi * k / n)), sign * float(np.sin(2 * np.pi * k / n))
    if k == 0:
        return value
    if 4 * k == n:
        return (None if im is None else im * -s, re * s)
    if im is None:
        return (re * c, re * s)
    return (re * c - im * s, re * s + im * c)


def plus(a, b):
    return a if b is None else b if a is None else a + b


def minus(a, b):
    return a if b is None else -b if a is None else a - b


def real_dft(x):
    n = len(x)
    if n == 1:
        return [(x[0], None)]
    if n == 2:
        return [(x[0] + x[1], None), (x[0] - x[1], None)]
    even, odd = real_dft(x[0::2]), real_dft(x[1::2])
    result = [None] * (n // 2 + 1)
    for k in range(n // 4 + 1):
        (er, ei), (orr, oi) = even[k], turned(odd[k], k, n, -1.0)
        result[k] = (plus(er, orr), plus(ei, oi))
        if 2 * k != n // 2:
            result[n // 2 - k] = (minus(er, orr), minus(oi, ei) if ei is not None or oi is not None else None)
    return result


def real_inverse(f, n):
    if n == 2:
        return [f[0][0] + f[1][0], f[0][0] - f[1][0]]
    even, odd = [], []
    for k in range(n // 4 + 1):
        (ar, ai), (br, bi) = f[k], f[n // 2 - k]
        if 2 * k == n // 2:
            even.append((ar + ar, None))
            odd.append((None if ai is None else -2.0 * ai, None))
            continue
        even.append((ar + br, None if k == 0 else minus(ai, bi)))
        odd.append(turned((ar - br, None if k == 0 else plus(ai, bi)), k, n, 1.0))
    result = [None] * n
    result[0::2] = real_inverse(even, n // 2)
    result[1::2] = real_inverse(odd, n // 2)
    return result


def split(value):
    high = value.astype(BF16)
    return high, (value - high.astype(F32)).astype(BF16)


def kernel(
    blocks,
    x_hbm,
    w_hbm,
    taps_hbm,
    h_hbm,
    gain_hbm,
    table_hbm,
    turn_hbm,
    out_ref,
    x_ref,
    taps_ref,
    h_ref,
    gain_ref,
    turn_ref,
    w_vm,
    table,
    part,
    relay,
    from_sum,
    from_one,
    fin,
    h_sent,
    h_got,
    u_kept,
    u_sent,
    u_got,
    y_sent,
    y_got,
    h_freq,
    work,
    w_sem,
    side_sem,
    far_send,
    far_recv,
    sum_send,
    sum_recv,
    here_sem,
    tile_send,
    tile_recv,
    rim_send,
    rim_recv,
    swap_send,
    swap_recv,
):
    me, row = lax.axis_index("ctx"), lax.axis_index("col")
    rows, wide = x_ref.shape[0], part.shape[3]
    chunks = rows // LANES
    per = wide // blocks
    freqs = blocks // 2 + 1
    half = freqs * per
    tiles = len(TILES)
    peers = blocks - 1
    levels = blocks.bit_length() - 2

    def at_col(offset):
        return (me, lax.rem(row + offset, 4))

    def peer(i):
        return lax.rem(me + i, blocks)

    def meet(level):
        if level > 0:
            pl.semaphore_wait(here_sem.at[level - 1], 2)
        if level < levels:
            for offset in (1 << level, blocks - (1 << level)):
                pl.semaphore_signal(here_sem.at[level], inc=1, device_id=(peer(offset), row), device_id_type=MESH)

    def weight_copy(t, o):
        j, g = TILES[t]
        start = pl.multiple_of(lax.rem(row + o, 4) * (2 * wide) + g * wide, LANES)
        return pltpu.make_async_copy(w_hbm.at[j, :, pl.ds(start, wide)], w_vm.at[t, o], w_sem.at[t, o])

    operands = ((x_hbm, x_ref), (h_hbm, h_ref), (taps_hbm, taps_ref), (table_hbm, table), (turn_hbm, turn_ref), (gain_hbm, gain_ref))
    x_copy, h_copy, *side_copies = [
        pltpu.make_async_copy(src, dst, side_sem.at[i]) for i, (src, dst) in enumerate(operands)
    ]
    x_copy.start()
    weight_copy(0, 2).start()
    weight_copy(1, 2).start()
    barrier = pltpu.get_barrier_semaphore()
    for offset in (1, 3):
        pl.semaphore_signal(barrier, inc=1, device_id=at_col(offset), device_id_type=MESH)
    for offset in (1, peers):
        pl.semaphore_signal(barrier, inc=1, device_id=(peer(offset), row), device_id_type=MESH)
    weight_copy(0, 3).start()
    weight_copy(1, 1).start()

    def fetch(pair):
        for order in ((2, 2), (3, 1), (1, 3), (0, 0)):
            for s in range(2):
                if pair > 0 or order[0] < 2:
                    weight_copy(2 * pair + s, order[s]).start()

    def project(t, o):
        pltpu.make_async_copy(w_vm.at[t, o], w_vm.at[t, o], w_sem.at[t, o]).wait()
        part[t, o] = jnp.dot(x_ref[...], w_vm[t, o], preferred_element_type=F32)

    def tile_copy(t, s, kind):
        onward, backward = 1 + 2 * s, 3 - 2 * s
        place, target, offset = ((2, relay, onward), (backward, from_one, backward))[kind]
        return pltpu.make_async_remote_copy(
            src_ref=part.at[t, place],
            dst_ref=target.at[t],
            send_sem=tile_send.at[kind, t],
            recv_sem=tile_recv.at[kind, t],
            device_id=at_col(offset),
            device_id_type=MESH,
        )

    def sum_copy(t, s, r):
        at = pl.ds(pl.multiple_of(r * LANES, LANES), LANES)
        return pltpu.make_async_remote_copy(
            src_ref=part.at[t, 1 + 2 * s, at],
            dst_ref=from_sum.at[t, at],
            send_sem=sum_send.at[t, r],
            recv_sem=sum_recv.at[t, r],
            device_id=at_col(1 + 2 * s),
            device_id_type=MESH,
        )

    def far_copy(t, s, r):
        at = pl.ds(pl.multiple_of(r * LANES, LANES), LANES)
        return pltpu.make_async_remote_copy(
            src_ref=part.at[t, 2, at],
            dst_ref=relay.at[t, at],
            send_sem=far_send.at[t, r],
            recv_sem=far_recv.at[t, r],
            device_id=at_col(1 + 2 * s),
            device_id_type=MESH,
        )

    def send_first():
        for s in range(2):
            pltpu.make_async_copy(w_vm.at[s, 2], w_vm.at[s, 2], w_sem.at[s, 2]).wait()

        @pl.loop(0, 2 * chunks)
        def _(i):
            r, s = i // 2, lax.rem(i, 2)
            at = pl.ds(pl.multiple_of(r * LANES, LANES), LANES)
            part[s, 2, at] = jnp.dot(x_ref[at, :], w_vm[s, 2], preferred_element_type=F32)

            @pl.when(i == 0)
            def _():
                pl.semaphore_wait(barrier, 4)

            far_copy(s, s, r).start()

    def send_far(pair):
        @pl.loop(0, 2)
        def _(s):
            project(2 * pair + s, 2)
            tile_copy(2 * pair + s, s, 0).start()

    def send_one(pair):
        @pl.loop(0, 2)
        def _(s):
            project(2 * pair + s, 3 - 2 * s)
            tile_copy(2 * pair + s, s, 1).start()

    def project_rest(pair):
        @pl.loop(0, 2)
        def _(s):
            project(2 * pair + s, 1 + 2 * s)
            project(2 * pair + s, 0)

    def send_sum(pair):
        if pair > 0:

            @pl.loop(0, 2)
            def _(s):
                tile_copy(2 * pair + s, s, 0).wait_recv()

        else:

            @pl.loop(0, chunks)
            def _(r):
                for s in range(2):
                    far_copy(s, s, r).wait_recv()

        @pl.loop(0, chunks)
        def _(i):
            r = chunks - 1 - i

            @pl.loop(0, 2)
            def _(s):
                t = 2 * pair + s
                at = pl.ds(pl.multiple_of(r * LANES, LANES), LANES)
                part[t, 1 + 2 * s, at] = part[t, 1 + 2 * s, at] + relay[t, at]
                sum_copy(t, s, r).start()

    def rim_copy(t):
        return pltpu.make_async_remote_copy(
            src_ref=fin.at[t, pl.ds(rows, RIM)],
            dst_ref=fin.at[t, pl.ds(0, RIM)],
            send_sem=rim_send.at[t],
            recv_sem=rim_recv.at[t],
            device_id=(peer(1), row),
            device_id_type=MESH,
        )

    def finish_chunk(pair, r):
        @pl.loop(0, 2)
        def _(s):
            t = 2 * pair + s
            sum_copy(t, s, r).wait_recv()
            at = pl.ds(pl.multiple_of(r * LANES, LANES), LANES)
            to = pl.ds(pl.multiple_of(r * LANES + RIM, RIM), LANES)
            fin[t, to] = part[t, 0, at] + from_sum[t, at] + from_one[t, at]

    def finish_last(pair):
        @pl.loop(0, 2)
        def _(s):
            tile_copy(2 * pair + s, s, 1).wait_recv()

        finish_chunk(pair, chunks - 1)

        @pl.loop(0, 2)
        def _(s):
            rim_copy(2 * pair + s).start()

    def finish_rim(pair):
        @pl.loop(0, 2)
        def _(s):
            rim_copy(2 * pair + s).wait_recv()

    def finish(pair):
        finish_last(pair)

        @pl.loop(1, chunks)
        def _(i):
            finish_chunk(pair, chunks - 1 - i)

        finish_rim(pair)

    def shaped(t, r):
        j, g = TILES[t]
        near = fin[t, pl.ds(pl.multiple_of(r * LANES, LANES), LANES + RIM)]
        tap = [taps_ref[i, j : j + 1, g * wide : (g + 1) * wide] for i in range(3)]
        return (
            tap[0] * near[RIM:] + tap[1] * near[RIM - 1 : RIM - 1 + LANES] + tap[2] * near[RIM - 2 : RIM - 2 + LANES]
        )

    def swap_start(which, g, source, target):
        @pl.loop(1, blocks)
        def _(i):
            p = peer(i)
            if which == 2:
                src, dst = source.at[g, p], target.at[g, pl.ds(pl.multiple_of(me * per, per), per)]
            else:
                src, dst = source.at[g, pl.ds(pl.multiple_of(p * per, per), per)], target.at[g, me]
            pltpu.make_async_remote_copy(
                src_ref=src,
                dst_ref=dst,
                send_sem=swap_send.at[which, g],
                recv_sem=swap_recv.at[which, g],
                device_id=(p, row),
                device_id_type=MESH,
            ).start()

        own = pl.ds(pl.multiple_of(me * per, per), per)
        if which == 2:
            target[g, own] = source[g, me]
        else:
            target[g, me] = source[g, own]

    def swap_wait(sem, which, g):
        held = h_got.at[0, pl.ds(0, peers)]
        pltpu.make_async_copy(held, held, sem.at[which, g]).wait()

    def times_tables(value):
        high, low = split(value)
        result = []
        for i in (0, 2):
            both = jnp.dot(jnp.concatenate([high, low], axis=0), table[i], preferred_element_type=F32)
            result.append(both[: 2 * half] + both[2 * half :] + jnp.dot(high, table[i + 1], preferred_element_type=F32))
        return result

    def spectrum(source, g):
        @pl.loop(0, chunks)
        def _(r):
            at = pl.ds(pl.multiple_of(r * LANES, LANES), LANES)
            found = real_dft([source[g, s, :, at] for s in range(blocks)])
            for k, (re, im) in enumerate(found):
                c, s = turn_ref[0, k : k + 1, at], turn_ref[1, k : k + 1, at]
                work[k * per : (k + 1) * per, at] = re * c if im is None else re * c + im * s
                work[half + k * per : half + (k + 1) * per, at] = -re * s if im is None else im * c - re * s

        by_cos, by_sin = times_tables(work[...])
        return by_cos[:half] + by_sin[half:], by_cos[half:] - by_sin[:half]

    def convolve(g):
        re, im = spectrum(u_got, g)
        h_re, h_im = h_freq[g, :half], h_freq[g, half:]
        product = jnp.concatenate([re * h_re - im * h_im, re * h_im + im * h_re], axis=0)
        by_cos, by_sin = times_tables(product)
        work[:half] = by_cos[:half] - by_sin[half:]
        work[half:] = by_cos[half:] + by_sin[:half]

        @pl.loop(0, chunks)
        def _(r):
            at = pl.ds(pl.multiple_of(r * LANES, LANES), LANES)
            freq = []
            for k in range(freqs):
                c, s = turn_ref[0, k : k + 1, at], turn_ref[1, k : k + 1, at]
                re, im = work[k * per : (k + 1) * per, at], work[half + k * per : half + (k + 1) * per, at]
                freq.append((re * c - im * s, None if k in (0, freqs - 1) else re * s + im * c))
            for s, value in enumerate(real_inverse(freq, blocks)):
                y_sent[g, s, :, at] = value

    def gate(g):
        for r in range(chunks):
            at = slice(r * LANES, (r + 1) * LANES)
            u = shaped(2 * g, r) * shaped(2 * g + 1, r)
            u_kept[g, at] = u
            u_sent[g, :, at] = u.T
        swap_start(1, g, u_sent, u_got)

    def through(g):
        swap_wait(swap_recv, 1, g)
        convolve(g)
        swap_start(2, g, y_sent, y_got)

    def sent(pair):
        @pl.loop(0, 2)
        def _(s):
            t = 2 * pair + s
            if pair > 0:
                tile_copy(t, s, 0).wait_send()
            tile_copy(t, s, 1).wait_send()
            rim_copy(t).wait_send()

            @pl.loop(0, chunks)
            def _(r):
                sum_copy(t, s, r).wait_send()

    def result(r):
        at = pl.ds(pl.multiple_of(r * LANES, LANES), LANES)
        for g in range(2):
            out_ref[at, g * wide : (g + 1) * wide] = shaped(4 + g, r) * u_kept[g, at]

    x_copy.wait()
    send_first()
    meet(0)
    send_one(0)
    h_copy.start()
    fetch(0)
    meet(1)
    fetch(1)
    h_copy.wait()
    for g in range(2):
        for r in range(chunks):
            at = slice(r * LANES, (r + 1) * LANES)
            h_sent[g, :, at] = h_ref[at, g * wide : (g + 1) * wide].T
    meet(2)
    project_rest(0)
    meet(3)
    for copy in side_copies:
        copy.start()
    send_sum(0)
    meet(4)
    for g in range(2):
        swap_start(0, g, h_sent, h_got)
    fetch(2)
    send_far(1)
    send_one(1)
    project_rest(1)
    for copy in side_copies:
        copy.wait()
    scale = 1.0 / (blocks * rows)
    for g in range(2):
        swap_wait(swap_recv, 0, g)

    @pl.loop(0, 2)
    def _(g):
        re, im = spectrum(h_got, g)
        h_freq[g, :half] = re * scale
        h_freq[g, half:] = im * scale

    finish(0)
    gate(0)
    send_sum(1)
    send_far(2)
    send_one(2)
    project_rest(2)
    through(0)
    finish(1)
    gate(1)
    send_sum(2)
    through(1)
    for g in range(2):
        swap_wait(swap_recv, 2, g)
        for r in range(chunks):
            at = slice(r * LANES, (r + 1) * LANES)
            u_kept[g, at] = y_got[g, :, at].T + gain_ref[:, g * wide : (g + 1) * wide] * u_kept[g, at]
    @pl.loop(0, chunks)
    def _(r):
        for s in range(2):
            far_copy(s, s, r).wait_send()

    sent(0)
    sent(1)
    for which in range(3):
        for g in range(2):
            swap_wait(swap_send, which, g)
    finish_last(2)

    @pl.loop(1, chunks)
    def _(i):
        r = chunks - 1 - i
        finish_chunk(2, r)
        result(r + 1)

    finish_rim(2)
    result(0)

    sent(2)


def on_device(blocks, sequence, w_proj, short_filter, long_filter, skip_gain):
    rows, depth = sequence.shape
    channels = long_filter.shape[1]
    wide = channels // 2
    per = wide // blocks
    freqs = blocks // 2 + 1
    tiles = len(TILES)
    *turn_tables, turn_cos, turn_sin = tables(blocks, rows)
    vmem = pl.BlockSpec(memory_space=pltpu.VMEM)
    hbm = pl.BlockSpec(memory_space=pl.ANY)
    tile = (tiles, rows, wide)
    sharded = (2, blocks, per, rows)
    flipped = (2, wide, rows)
    return pl.pallas_call(
        functools.partial(kernel, blocks),
        out_shape=pltpu.VMEM((rows, channels), F32),
        in_specs=[hbm] * 7,
        out_specs=vmem,
        scratch_shapes=[
            pltpu.VMEM((rows, depth), BF16),
            pltpu.VMEM(short_filter.shape, F32),
            pltpu.VMEM((rows, channels), F32),
            pltpu.VMEM((1, channels), F32),
            pltpu.VMEM((2, freqs, rows), F32),
            pltpu.VMEM((tiles, 4, depth, wide), BF16),
            pltpu.VMEM((4, rows, rows), BF16),
            pltpu.VMEM((tiles, 4, rows, wide), F32),
            pltpu.VMEM(tile, F32),
            pltpu.VMEM(tile, F32),
            pltpu.VMEM(tile, F32),
            pltpu.VMEM((tiles, rows + RIM, wide), F32),
            pltpu.VMEM(flipped, F32),
            pltpu.VMEM(sharded, F32),
            pltpu.VMEM((2, rows, wide), F32),
            pltpu.VMEM(flipped, F32),
            pltpu.VMEM(sharded, F32),
            pltpu.VMEM(sharded, F32),
            pltpu.VMEM(flipped, F32),
            pltpu.VMEM((2, 2 * freqs * per, rows), F32),
            pltpu.VMEM((2 * freqs * per, rows), F32),
            pltpu.SemaphoreType.DMA((tiles, 4)),
            pltpu.SemaphoreType.DMA((6,)),
            pltpu.SemaphoreType.DMA((2, rows // LANES)),
            pltpu.SemaphoreType.DMA((2, rows // LANES)),
            pltpu.SemaphoreType.DMA((tiles, rows // LANES)),
            pltpu.SemaphoreType.DMA((tiles, rows // LANES)),
            pltpu.SemaphoreType.REGULAR((blocks.bit_length() - 2,)),
            pltpu.SemaphoreType.DMA((2, tiles)),
            pltpu.SemaphoreType.DMA((2, tiles)),
            pltpu.SemaphoreType.DMA((tiles,)),
            pltpu.SemaphoreType.DMA((tiles,)),
            pltpu.SemaphoreType.DMA((3, 2)),
            pltpu.SemaphoreType.DMA((3, 2)),
        ],
        compiler_params=pltpu.CompilerParams(
            collective_id=0, has_side_effects=True, vmem_limit_bytes=56 << 20
        ),
        cost_estimate=pl.CostEstimate(
            flops=2 * rows * depth * 12 * channels, bytes_accessed=16 << 20, transcendentals=0
        ),
    )(
        sequence,
        w_proj.transpose(1, 0, 2),
        short_filter,
        long_filter,
        skip_gain[None, :],
        np.stack(turn_tables),
        np.stack([turn_cos, turn_sin]),
    )


def solution(mesh):
    return jax.shard_map(
        functools.partial(on_device, mesh.shape["ctx"]),
        mesh=mesh,
        in_specs=(
            P("ctx", "col"),
            P("col", None, None),
            P(None, None, "col"),
            P("ctx", "col"),
            P("col"),
        ),
        out_specs=P("ctx", "col"),
        check_vma=False,
    )
```

```python
import functools

import ml_dtypes
import numpy as np

import jax
import jax.numpy as jnp
from jax import lax
from jax.experimental import pallas as pl
from jax.experimental.pallas import tpu as pltpu
from jax.sharding import PartitionSpec as P

MESH = pl.DeviceIdType.MESH
F32 = jnp.float32
BF16 = jnp.bfloat16
LANES = 128
RIM = 8

TILES = ((1, 0), (2, 0), (1, 1), (2, 1), (0, 0), (0, 1))


def tables(blocks, rows):
    outer, inner = np.arange(blocks // 2 + 1), np.arange(rows)
    turn = 2 * np.pi / (blocks * rows) * (outer[:, None] * inner[None, :] % (blocks * rows))
    angle = 2 * np.pi / rows * (inner[:, None] * inner[None, :] % rows)
    result = []
    for full in (np.cos(angle), np.sin(angle)):
        high = full.astype(ml_dtypes.bfloat16)
        result += [high, (full - high.astype(np.float64)).astype(ml_dtypes.bfloat16)]
    return result + [np.cos(turn).astype(np.float32), np.sin(turn).astype(np.float32)]


def scaled(value, factor):
    return value if factor == 1.0 else value * factor


def turned(value, k, n, sign):
    re, im = value
    c, s = float(np.cos(2 * np.pi * k / n)), sign * float(np.sin(2 * np.pi * k / n))
    if k == 0:
        return value
    if 4 * k == n:
        return (None if im is None else im * -s, re * s)
    if im is None:
        return (re * c, re * s)
    return (re * c - im * s, re * s + im * c)


def plus(a, b):
    return a if b is None else b if a is None else a + b


def minus(a, b):
    return a if b is None else -b if a is None else a - b


def real_dft(x):
    n = len(x)
    if n == 1:
        return [(x[0], None)]
    if n == 2:
        return [(x[0] + x[1], None), (x[0] - x[1], None)]
    even, odd = real_dft(x[0::2]), real_dft(x[1::2])
    result = [None] * (n // 2 + 1)
    for k in range(n // 4 + 1):
        (er, ei), (orr, oi) = even[k], turned(odd[k], k, n, -1.0)
        result[k] = (plus(er, orr), plus(ei, oi))
        if 2 * k != n // 2:
            result[n // 2 - k] = (minus(er, orr), minus(oi, ei) if ei is not None or oi is not None else None)
    return result


def real_inverse(f, n):
    if n == 2:
        return [f[0][0] + f[1][0], f[0][0] - f[1][0]]
    even, odd = [], []
    for k in range(n // 4 + 1):
        (ar, ai), (br, bi) = f[k], f[n // 2 - k]
        if 2 * k == n // 2:
            even.append((ar + ar, None))
            odd.append((None if ai is None else -2.0 * ai, None))
            continue
        even.append((ar + br, None if k == 0 else minus(ai, bi)))
        odd.append(turned((ar - br, None if k == 0 else plus(ai, bi)), k, n, 1.0))
    result = [None] * n
    result[0::2] = real_inverse(even, n // 2)
    result[1::2] = real_inverse(odd, n // 2)
    return result


def split(value):
    high = value.astype(BF16)
    return high, (value - high.astype(F32)).astype(BF16)


def kernel(
    blocks,
    x_hbm,
    w_hbm,
    taps_hbm,
    h_hbm,
    gain_hbm,
    table_hbm,
    turn_hbm,
    out_ref,
    x_ref,
    taps_ref,
    h_ref,
    gain_ref,
    turn_ref,
    w_vm,
    table,
    part,
    relay,
    from_sum,
    from_one,
    fin,
    h_sent,
    h_got,
    u_kept,
    u_sent,
    u_got,
    y_sent,
    y_got,
    h_freq,
    work,
    w_sem,
    x_sem,
    side_sem,
    far_send,
    far_recv,
    sum_send,
    sum_recv,
    here_sem,
    tile_send,
    tile_recv,
    rim_send,
    rim_recv,
    swap_send,
    swap_recv,
):
    me, row = lax.axis_index("ctx"), lax.axis_index("col")
    rows, wide = x_ref.shape[0], part.shape[3]
    chunks = rows // LANES
    per = wide // blocks
    freqs = blocks // 2 + 1
    half = freqs * per
    tiles = len(TILES)
    peers = blocks - 1
    levels = blocks.bit_length() - 1

    def at_col(offset):
        return (me, lax.rem(row + offset, 4))

    def peer(i):
        return lax.rem(me + i, blocks)

    def meet(level):
        def tell(offset):
            pl.semaphore_signal(
                here_sem.at[level], inc=1, device_id=(peer(offset), row), device_id_type=MESH
            )

        if level > 0:
            pl.semaphore_wait(here_sem.at[level - 1], 1 if level == 1 else 2)
        if level == 0:
            tell(peers)
        elif level < levels:
            tell(1 << (level - 1))
            tell(blocks - (1 << (level - 1)))

    def weight_copy(t, o):
        j, g = TILES[t]
        start = pl.multiple_of(lax.rem(row + o, 4) * (2 * wide) + g * wide, LANES)
        return pltpu.make_async_copy(w_hbm.at[j, :, pl.ds(start, wide)], w_vm.at[t, o], w_sem.at[t, o])

    def x_copy(r):
        at = pl.ds(pl.multiple_of(r * LANES, LANES), LANES)
        return pltpu.make_async_copy(x_hbm.at[at], x_ref.at[at], x_sem.at[r])

    def weight_pieces(t, o):
        j, g = TILES[t]
        start = pl.multiple_of(lax.rem(row + o, 4) * (2 * wide) + g * wide, LANES)
        deep = x_ref.shape[1] // 4
        for i in range(4):
            at = pl.ds(i * deep, deep)
            pltpu.make_async_copy(w_hbm.at[j, at, pl.ds(start, wide)], w_vm.at[t, o, at], w_sem.at[t, o]).start()

    operands = ((h_hbm, h_ref), (taps_hbm, taps_ref), (table_hbm, table), (turn_hbm, turn_ref), (gain_hbm, gain_ref))
    h_copy, *side_copies = [
        pltpu.make_async_copy(src, dst, side_sem.at[i]) for i, (src, dst) in enumerate(operands)
    ]
    x_copy(0).start()
    weight_pieces(0, 2)
    weight_pieces(1, 2)
    for r in range(1, chunks):
        x_copy(r).start()
    barrier = pltpu.get_barrier_semaphore()
    for offset in (1, 3):
        pl.semaphore_signal(barrier, inc=1, device_id=at_col(offset), device_id_type=MESH)
    pl.semaphore_signal(barrier, inc=1, device_id=(peer(1), row), device_id_type=MESH)
    weight_copy(0, 3).start()
    weight_copy(1, 1).start()

    def fetch(pair):
        for order in ((2, 2), (3, 1), (1, 3), (0, 0)):
            for s in range(2):
                if pair > 0 or order[0] < 2:
                    weight_copy(2 * pair + s, order[s]).start()

    def project(t, o):
        pltpu.make_async_copy(w_vm.at[t, o], w_vm.at[t, o], w_sem.at[t, o]).wait()
        part[t, o] = jnp.dot(x_ref[...], w_vm[t, o], preferred_element_type=F32)

    def tile_copy(t, s, kind):
        onward, backward = 1 + 2 * s, 3 - 2 * s
        place, target, offset = ((2, relay, onward), (backward, from_one, backward))[kind]
        return pltpu.make_async_remote_copy(
            src_ref=part.at[t, place],
            dst_ref=target.at[t],
            send_sem=tile_send.at[kind, t],
            recv_sem=tile_recv.at[kind, t],
            device_id=at_col(offset),
            device_id_type=MESH,
        )

    def sum_copy(t, s, r):
        at = pl.ds(pl.multiple_of(r * LANES, LANES), LANES)
        return pltpu.make_async_remote_copy(
            src_ref=part.at[t, 1 + 2 * s, at],
            dst_ref=from_sum.at[t, at],
            send_sem=sum_send.at[t, r],
            recv_sem=sum_recv.at[t, r],
            device_id=at_col(1 + 2 * s),
            device_id_type=MESH,
        )

    def far_copy(t, s, r):
        at = pl.ds(pl.multiple_of(r * LANES, LANES), LANES)
        return pltpu.make_async_remote_copy(
            src_ref=part.at[t, 2, at],
            dst_ref=relay.at[t, at],
            send_sem=far_send.at[t, r],
            recv_sem=far_recv.at[t, r],
            device_id=at_col(1 + 2 * s),
            device_id_type=MESH,
        )

    def send_first():
        @pl.loop(0, 2 * chunks)
        def _(i):
            r, s = i // 2, lax.rem(i, 2)
            at = pl.ds(pl.multiple_of(r * LANES, LANES), LANES)

            @pl.when(r == 0)
            def _():
                pltpu.make_async_copy(w_vm.at[s, 2], w_vm.at[s, 2], w_sem.at[s, 2]).wait()

            @pl.when(s == 0)
            def _():
                x_copy(r).wait()

            part[s, 2, at] = jnp.dot(x_ref[at, :], w_vm[s, 2], preferred_element_type=F32)

            @pl.when(i == 0)
            def _():
                pl.semaphore_wait(barrier, 3)

            far_copy(s, s, r).start()

    def send_far(pair):
        @pl.loop(0, 2)
        def _(s):
            project(2 * pair + s, 2)
            tile_copy(2 * pair + s, s, 0).start()

    def send_one(pair):
        @pl.loop(0, 2)
        def _(s):
            project(2 * pair + s, 3 - 2 * s)
            tile_copy(2 * pair + s, s, 1).start()

    def project_rest(pair):
        @pl.loop(0, 2)
        def _(s):
            project(2 * pair + s, 1 + 2 * s)
            project(2 * pair + s, 0)

    def send_sum(pair):
        if pair > 0:

            @pl.loop(0, 2)
            def _(s):
                tile_copy(2 * pair + s, s, 0).wait_recv()

        else:

            @pl.loop(0, chunks)
            def _(r):
                for s in range(2):
                    far_copy(s, s, r).wait_recv()

        @pl.loop(0, chunks)
        def _(i):
            r = chunks - 1 - i

            @pl.loop(0, 2)
            def _(s):
                t = 2 * pair + s
                at = pl.ds(pl.multiple_of(r * LANES, LANES), LANES)
                part[t, 1 + 2 * s, at] = part[t, 1 + 2 * s, at] + relay[t, at]
                sum_copy(t, s, r).start()

    def rim_copy(t):
        return pltpu.make_async_remote_copy(
            src_ref=fin.at[t, pl.ds(rows, RIM)],
            dst_ref=fin.at[t, pl.ds(0, RIM)],
            send_sem=rim_send.at[t],
            recv_sem=rim_recv.at[t],
            device_id=(peer(1), row),
            device_id_type=MESH,
        )

    def finish_chunk(pair, r):
        @pl.loop(0, 2)
        def _(s):
            t = 2 * pair + s
            sum_copy(t, s, r).wait_recv()
            at = pl.ds(pl.multiple_of(r * LANES, LANES), LANES)
            to = pl.ds(pl.multiple_of(r * LANES + RIM, RIM), LANES)
            fin[t, to] = part[t, 0, at] + from_sum[t, at] + from_one[t, at]

    def finish_last(pair):
        @pl.loop(0, 2)
        def _(s):
            tile_copy(2 * pair + s, s, 1).wait_recv()

        finish_chunk(pair, chunks - 1)

        @pl.loop(0, 2)
        def _(s):
            rim_copy(2 * pair + s).start()

    def finish_rim(pair):
        @pl.loop(0, 2)
        def _(s):
            rim_copy(2 * pair + s).wait_recv()

    def finish(pair):
        finish_last(pair)

        @pl.loop(1, chunks)
        def _(i):
            finish_chunk(pair, chunks - 1 - i)

        finish_rim(pair)

    def shaped(t, r):
        j, g = TILES[t]
        near = fin[t, pl.ds(pl.multiple_of(r * LANES, LANES), LANES + RIM)]
        tap = [taps_ref[i, j : j + 1, g * wide : (g + 1) * wide] for i in range(3)]
        return (
            tap[0] * near[RIM:] + tap[1] * near[RIM - 1 : RIM - 1 + LANES] + tap[2] * near[RIM - 2 : RIM - 2 + LANES]
        )

    def swap_start(which, g, source, target):
        @pl.loop(1, blocks)
        def _(i):
            p = peer(i)
            if which == 2:
                src, dst = source.at[g, p], target.at[g, pl.ds(pl.multiple_of(me * per, per), per)]
            else:
                src, dst = source.at[g, pl.ds(pl.multiple_of(p * per, per), per)], target.at[g, me]
            pltpu.make_async_remote_copy(
                src_ref=src,
                dst_ref=dst,
                send_sem=swap_send.at[which, g],
                recv_sem=swap_recv.at[which, g],
                device_id=(p, row),
                device_id_type=MESH,
            ).start()

        own = pl.ds(pl.multiple_of(me * per, per), per)
        if which == 2:
            target[g, own] = source[g, me]
        else:
            target[g, me] = source[g, own]

    def swap_wait(sem, which, g):
        held = h_got.at[0, pl.ds(0, peers)]
        pltpu.make_async_copy(held, held, sem.at[which, g]).wait()

    def times_tables(value):
        high, low = split(value)
        result = []
        for i in (0, 2):
            both = jnp.dot(jnp.concatenate([high, low], axis=0), table[i], preferred_element_type=F32)
            result.append(both[: 2 * half] + both[2 * half :] + jnp.dot(high, table[i + 1], preferred_element_type=F32))
        return result

    def spectrum(source, g):
        @pl.loop(0, chunks)
        def _(r):
            at = pl.ds(pl.multiple_of(r * LANES, LANES), LANES)
            found = real_dft([source[g, s, :, at] for s in range(blocks)])
            for k, (re, im) in enumerate(found):
                c, s = turn_ref[0, k : k + 1, at], turn_ref[1, k : k + 1, at]
                work[k * per : (k + 1) * per, at] = re * c if im is None else re * c + im * s
                work[half + k * per : half + (k + 1) * per, at] = -re * s if im is None else im * c - re * s

        by_cos, by_sin = times_tables(work[...])
        return by_cos[:half] + by_sin[half:], by_cos[half:] - by_sin[:half]

    def convolve(g):
        re, im = spectrum(u_got, g)
        h_re, h_im = h_freq[g, :half], h_freq[g, half:]
        product = jnp.concatenate([re * h_re - im * h_im, re * h_im + im * h_re], axis=0)
        by_cos, by_sin = times_tables(product)
        work[:half] = by_cos[:half] - by_sin[half:]
        work[half:] = by_cos[half:] + by_sin[:half]

        @pl.loop(0, chunks)
        def _(r):
            at = pl.ds(pl.multiple_of(r * LANES, LANES), LANES)
            freq = []
            for k in range(freqs):
                c, s = turn_ref[0, k : k + 1, at], turn_ref[1, k : k + 1, at]
                re, im = work[k * per : (k + 1) * per, at], work[half + k * per : half + (k + 1) * per, at]
                freq.append((re * c - im * s, None if k in (0, freqs - 1) else re * s + im * c))
            for s, value in enumerate(real_inverse(freq, blocks)):
                y_sent[g, s, :, at] = value

    def gate(g):
        for r in range(chunks):
            at = slice(r * LANES, (r + 1) * LANES)
            u = shaped(2 * g, r) * shaped(2 * g + 1, r)
            u_kept[g, at] = u
            u_sent[g, :, at] = u.T
        swap_start(1, g, u_sent, u_got)

    def through(g):
        swap_wait(swap_recv, 1, g)
        convolve(g)
        swap_start(2, g, y_sent, y_got)

    def sent(pair):
        @pl.loop(0, 2)
        def _(s):
            t = 2 * pair + s
            if pair > 0:
                tile_copy(t, s, 0).wait_send()
            tile_copy(t, s, 1).wait_send()
            rim_copy(t).wait_send()

            @pl.loop(0, chunks)
            def _(r):
                sum_copy(t, s, r).wait_send()

    def result(r):
        at = pl.ds(pl.multiple_of(r * LANES, LANES), LANES)
        for g in range(2):
            out_ref[at, g * wide : (g + 1) * wide] = shaped(4 + g, r) * u_kept[g, at]

    send_first()
    meet(0)
    meet(1)
    send_one(0)
    h_copy.start()
    fetch(0)
    meet(2)
    fetch(1)
    h_copy.wait()
    for g in range(2):
        for r in range(chunks):
            at = slice(r * LANES, (r + 1) * LANES)
            h_sent[g, :, at] = h_ref[at, g * wide : (g + 1) * wide].T
    meet(3)
    project_rest(0)
    meet(4)
    for copy in side_copies:
        copy.start()
    send_sum(0)
    meet(5)
    for g in range(2):
        swap_start(0, g, h_sent, h_got)
    fetch(2)
    send_far(1)
    send_one(1)
    project_rest(1)
    for copy in side_copies:
        copy.wait()
    scale = 1.0 / (blocks * rows)
    for g in range(2):
        swap_wait(swap_recv, 0, g)

    @pl.loop(0, 2)
    def _(g):
        re, im = spectrum(h_got, g)
        h_freq[g, :half] = re * scale
        h_freq[g, half:] = im * scale

    finish(0)
    gate(0)
    send_sum(1)
    send_far(2)
    send_one(2)
    project_rest(2)
    through(0)
    finish(1)
    gate(1)
    send_sum(2)
    through(1)
    for g in range(2):
        swap_wait(swap_recv, 2, g)
        for r in range(chunks):
            at = slice(r * LANES, (r + 1) * LANES)
            u_kept[g, at] = y_got[g, :, at].T + gain_ref[:, g * wide : (g + 1) * wide] * u_kept[g, at]
    @pl.loop(0, chunks)
    def _(r):
        for s in range(2):
            far_copy(s, s, r).wait_send()

    sent(0)
    sent(1)
    for which in range(3):
        for g in range(2):
            swap_wait(swap_send, which, g)
    finish_last(2)

    @pl.loop(1, chunks)
    def _(i):
        r = chunks - 1 - i
        finish_chunk(2, r)
        result(r + 1)

    finish_rim(2)
    result(0)

    sent(2)


def on_device(blocks, sequence, w_proj, short_filter, long_filter, skip_gain):
    rows, depth = sequence.shape
    channels = long_filter.shape[1]
    wide = channels // 2
    per = wide // blocks
    freqs = blocks // 2 + 1
    tiles = len(TILES)
    *turn_tables, turn_cos, turn_sin = tables(blocks, rows)
    vmem = pl.BlockSpec(memory_space=pltpu.VMEM)
    hbm = pl.BlockSpec(memory_space=pl.ANY)
    tile = (tiles, rows, wide)
    sharded = (2, blocks, per, rows)
    flipped = (2, wide, rows)
    return pl.pallas_call(
        functools.partial(kernel, blocks),
        out_shape=pltpu.VMEM((rows, channels), F32),
        in_specs=[hbm] * 7,
        out_specs=vmem,
        scratch_shapes=[
            pltpu.VMEM((rows, depth), BF16),
            pltpu.VMEM(short_filter.shape, F32),
            pltpu.VMEM((rows, channels), F32),
            pltpu.VMEM((1, channels), F32),
            pltpu.VMEM((2, freqs, rows), F32),
            pltpu.VMEM((tiles, 4, depth, wide), BF16),
            pltpu.VMEM((4, rows, rows), BF16),
            pltpu.VMEM((tiles, 4, rows, wide), F32),
            pltpu.VMEM(tile, F32),
            pltpu.VMEM(tile, F32),
            pltpu.VMEM(tile, F32),
            pltpu.VMEM((tiles, rows + RIM, wide), F32),
            pltpu.VMEM(flipped, F32),
            pltpu.VMEM(sharded, F32),
            pltpu.VMEM((2, rows, wide), F32),
            pltpu.VMEM(flipped, F32),
            pltpu.VMEM(sharded, F32),
            pltpu.VMEM(sharded, F32),
            pltpu.VMEM(flipped, F32),
            pltpu.VMEM((2, 2 * freqs * per, rows), F32),
            pltpu.VMEM((2 * freqs * per, rows), F32),
            pltpu.SemaphoreType.DMA((tiles, 4)),
            pltpu.SemaphoreType.DMA((rows // LANES,)),
            pltpu.SemaphoreType.DMA((5,)),
            pltpu.SemaphoreType.DMA((2, rows // LANES)),
            pltpu.SemaphoreType.DMA((2, rows // LANES)),
            pltpu.SemaphoreType.DMA((tiles, rows // LANES)),
            pltpu.SemaphoreType.DMA((tiles, rows // LANES)),
            pltpu.SemaphoreType.REGULAR((blocks.bit_length() - 1,)),
            pltpu.SemaphoreType.DMA((2, tiles)),
            pltpu.SemaphoreType.DMA((2, tiles)),
            pltpu.SemaphoreType.DMA((tiles,)),
            pltpu.SemaphoreType.DMA((tiles,)),
            pltpu.SemaphoreType.DMA((3, 2)),
            pltpu.SemaphoreType.DMA((3, 2)),
        ],
        compiler_params=pltpu.CompilerParams(
            collective_id=0, has_side_effects=True, vmem_limit_bytes=56 << 20
        ),
        cost_estimate=pl.CostEstimate(
            flops=2 * rows * depth * 12 * channels, bytes_accessed=16 << 20, transcendentals=0
        ),
    )(
        sequence,
        w_proj.transpose(1, 0, 2),
        short_filter,
        long_filter,
        skip_gain[None, :],
        np.stack(turn_tables),
        np.stack([turn_cos, turn_sin]),
    )


def solution(mesh):
    return jax.shard_map(
        functools.partial(on_device, mesh.shape["ctx"]),
        mesh=mesh,
        in_specs=(
            P("ctx", "col"),
            P("col", None, None),
            P(None, None, "col"),
            P("ctx", "col"),
            P("col"),
        ),
        out_specs=P("ctx", "col"),
        check_vma=False,
    )
```

```python
import functools

import ml_dtypes
import numpy as np

import jax
import jax.numpy as jnp
from jax import lax
from jax.experimental import pallas as pl
from jax.experimental.pallas import tpu as pltpu
from jax.sharding import PartitionSpec as P

MESH = pl.DeviceIdType.MESH
F32 = jnp.float32
BF16 = jnp.bfloat16
LANES = 128
RIM = 8

TILES = ((1, 0), (2, 0), (1, 1), (2, 1), (0, 0), (0, 1))


def tables(blocks, rows):
    outer, inner = np.arange(blocks // 2 + 1), np.arange(rows)
    turn = 2 * np.pi / (blocks * rows) * (outer[:, None] * inner[None, :] % (blocks * rows))
    angle = 2 * np.pi / rows * (inner[:, None] * inner[None, :] % rows)
    result = []
    for full in (np.cos(angle), np.sin(angle)):
        high = full.astype(ml_dtypes.bfloat16)
        result += [high, (full - high.astype(np.float64)).astype(ml_dtypes.bfloat16)]
    return result + [np.cos(turn).astype(np.float32), np.sin(turn).astype(np.float32)]


def scaled(value, factor):
    return value if factor == 1.0 else value * factor


def turned(value, k, n, sign):
    re, im = value
    c, s = float(np.cos(2 * np.pi * k / n)), sign * float(np.sin(2 * np.pi * k / n))
    if k == 0:
        return value
    if 4 * k == n:
        return (None if im is None else im * -s, re * s)
    if im is None:
        return (re * c, re * s)
    return (re * c - im * s, re * s + im * c)


def plus(a, b):
    return a if b is None else b if a is None else a + b


def minus(a, b):
    return a if b is None else -b if a is None else a - b


def real_dft(x):
    n = len(x)
    if n == 1:
        return [(x[0], None)]
    if n == 2:
        return [(x[0] + x[1], None), (x[0] - x[1], None)]
    even, odd = real_dft(x[0::2]), real_dft(x[1::2])
    result = [None] * (n // 2 + 1)
    for k in range(n // 4 + 1):
        (er, ei), (orr, oi) = even[k], turned(odd[k], k, n, -1.0)
        result[k] = (plus(er, orr), plus(ei, oi))
        if 2 * k != n // 2:
            result[n // 2 - k] = (minus(er, orr), minus(oi, ei) if ei is not None or oi is not None else None)
    return result


def real_inverse(f, n):
    if n == 2:
        return [f[0][0] + f[1][0], f[0][0] - f[1][0]]
    even, odd = [], []
    for k in range(n // 4 + 1):
        (ar, ai), (br, bi) = f[k], f[n // 2 - k]
        if 2 * k == n // 2:
            even.append((ar + ar, None))
            odd.append((None if ai is None else -2.0 * ai, None))
            continue
        even.append((ar + br, None if k == 0 else minus(ai, bi)))
        odd.append(turned((ar - br, None if k == 0 else plus(ai, bi)), k, n, 1.0))
    result = [None] * n
    result[0::2] = real_inverse(even, n // 2)
    result[1::2] = real_inverse(odd, n // 2)
    return result


def split(value):
    high = value.astype(BF16)
    return high, (value - high.astype(F32)).astype(BF16)


def kernel(
    blocks,
    x_hbm,
    w_hbm,
    taps_hbm,
    h_hbm,
    gain_hbm,
    table_hbm,
    turn_hbm,
    out_ref,
    x_ref,
    taps_ref,
    h_ref,
    gain_ref,
    turn_ref,
    w_vm,
    table,
    part,
    relay,
    from_sum,
    from_one,
    fin,
    h_sent,
    h_got,
    u_kept,
    u_sent,
    u_got,
    y_sent,
    y_got,
    h_freq,
    work,
    w_sem,
    x_sem,
    side_sem,
    far_send,
    far_recv,
    sum_send,
    sum_recv,
    here_sem,
    tile_send,
    tile_recv,
    rim_send,
    rim_recv,
    swap_send,
    swap_recv,
):
    me, row = lax.axis_index("ctx"), lax.axis_index("col")
    rows, wide = x_ref.shape[0], part.shape[3]
    chunks = rows // LANES
    per = wide // blocks
    freqs = blocks // 2 + 1
    half = freqs * per
    tiles = len(TILES)
    peers = blocks - 1
    levels = blocks.bit_length() - 1

    def at_col(offset):
        return (me, lax.rem(row + offset, 4))

    def peer(i):
        return lax.rem(me + i, blocks)

    def meet(level):
        def tell(offset):
            pl.semaphore_signal(
                here_sem.at[level], inc=1, device_id=(peer(offset), row), device_id_type=MESH
            )

        if level > 0:
            pl.semaphore_wait(here_sem.at[level - 1], 1 if level == 1 else 2)
        if level == 0:
            tell(peers)
        elif level < levels:
            tell(1 << (level - 1))
            tell(blocks - (1 << (level - 1)))

    def weight_copy(t, o):
        j, g = TILES[t]
        start = pl.multiple_of(lax.rem(row + o, 4) * (2 * wide) + g * wide, LANES)
        return pltpu.make_async_copy(w_hbm.at[j, :, pl.ds(start, wide)], w_vm.at[t, o], w_sem.at[t, o])

    def x_copy(r):
        at = pl.ds(pl.multiple_of(r * LANES, LANES), LANES)
        return pltpu.make_async_copy(x_hbm.at[at], x_ref.at[at], x_sem.at[r])

    def weight_pieces(t, o):
        j, g = TILES[t]
        start = pl.multiple_of(lax.rem(row + o, 4) * (2 * wide) + g * wide, LANES)
        deep = x_ref.shape[1] // 4
        for i in range(4):
            at = pl.ds(i * deep, deep)
            pltpu.make_async_copy(w_hbm.at[j, at, pl.ds(start, wide)], w_vm.at[t, o, at], w_sem.at[t, o]).start()

    operands = ((h_hbm, h_ref), (taps_hbm, taps_ref), (table_hbm, table), (turn_hbm, turn_ref), (gain_hbm, gain_ref))
    h_copy, *side_copies = [
        pltpu.make_async_copy(src, dst, side_sem.at[i]) for i, (src, dst) in enumerate(operands)
    ]
    barrier = pltpu.get_barrier_semaphore()
    for offset in (1, 3):
        pl.semaphore_signal(barrier, inc=1, device_id=at_col(offset), device_id_type=MESH)
    pl.semaphore_signal(barrier, inc=1, device_id=(peer(1), row), device_id_type=MESH)
    x_copy(0).start()
    weight_pieces(0, 2)
    weight_pieces(1, 2)
    for r in range(1, chunks):
        x_copy(r).start()
    weight_copy(0, 3).start()
    weight_copy(1, 1).start()

    def fetch(pair):
        for order in ((2, 2), (3, 1), (1, 3), (0, 0)):
            for s in range(2):
                if pair > 0 or order[0] < 2:
                    weight_copy(2 * pair + s, order[s]).start()

    def project(t, o):
        pltpu.make_async_copy(w_vm.at[t, o], w_vm.at[t, o], w_sem.at[t, o]).wait()
        part[t, o] = jnp.dot(x_ref[...], w_vm[t, o], preferred_element_type=F32)

    def tile_copy(t, s, kind):
        onward, backward = 1 + 2 * s, 3 - 2 * s
        place, target, offset = ((2, relay, onward), (backward, from_one, backward))[kind]
        return pltpu.make_async_remote_copy(
            src_ref=part.at[t, place],
            dst_ref=target.at[t],
            send_sem=tile_send.at[kind, t],
            recv_sem=tile_recv.at[kind, t],
            device_id=at_col(offset),
            device_id_type=MESH,
        )

    def sum_copy(t, s, r):
        at = pl.ds(pl.multiple_of(r * LANES, LANES), LANES)
        return pltpu.make_async_remote_copy(
            src_ref=part.at[t, 1 + 2 * s, at],
            dst_ref=from_sum.at[t, at],
            send_sem=sum_send.at[t, r],
            recv_sem=sum_recv.at[t, r],
            device_id=at_col(1 + 2 * s),
            device_id_type=MESH,
        )

    def far_copy(t, s, r):
        at = pl.ds(pl.multiple_of(r * LANES, LANES), LANES)
        return pltpu.make_async_remote_copy(
            src_ref=part.at[t, 2, at],
            dst_ref=relay.at[t, at],
            send_sem=far_send.at[t, r],
            recv_sem=far_recv.at[t, r],
            device_id=at_col(1 + 2 * s),
            device_id_type=MESH,
        )

    def send_first():
        @pl.loop(0, 2 * chunks)
        def _(i):
            r, s = i // 2, lax.rem(i, 2)
            at = pl.ds(pl.multiple_of(r * LANES, LANES), LANES)

            @pl.when(r == 0)
            def _():
                pltpu.make_async_copy(w_vm.at[s, 2], w_vm.at[s, 2], w_sem.at[s, 2]).wait()

            @pl.when(s == 0)
            def _():
                x_copy(r).wait()

            part[s, 2, at] = jnp.dot(x_ref[at, :], w_vm[s, 2], preferred_element_type=F32)

            @pl.when(i == 0)
            def _():
                pl.semaphore_wait(barrier, 3)

            far_copy(s, s, r).start()

    def send_far(pair):
        @pl.loop(0, 2)
        def _(s):
            project(2 * pair + s, 2)
            tile_copy(2 * pair + s, s, 0).start()

    def send_one(pair):
        @pl.loop(0, 2)
        def _(s):
            project(2 * pair + s, 3 - 2 * s)
            tile_copy(2 * pair + s, s, 1).start()

    def project_rest(pair):
        @pl.loop(0, 2)
        def _(s):
            project(2 * pair + s, 1 + 2 * s)
            project(2 * pair + s, 0)

    def send_sum(pair):
        if pair > 0:

            @pl.loop(0, 2)
            def _(s):
                tile_copy(2 * pair + s, s, 0).wait_recv()

        else:

            @pl.loop(0, chunks)
            def _(r):
                for s in range(2):
                    far_copy(s, s, r).wait_recv()

        @pl.loop(0, chunks)
        def _(i):
            r = chunks - 1 - i

            @pl.loop(0, 2)
            def _(s):
                t = 2 * pair + s
                at = pl.ds(pl.multiple_of(r * LANES, LANES), LANES)
                part[t, 1 + 2 * s, at] = part[t, 1 + 2 * s, at] + relay[t, at]
                sum_copy(t, s, r).start()

    def rim_copy(t):
        return pltpu.make_async_remote_copy(
            src_ref=fin.at[t, pl.ds(rows, RIM)],
            dst_ref=fin.at[t, pl.ds(0, RIM)],
            send_sem=rim_send.at[t],
            recv_sem=rim_recv.at[t],
            device_id=(peer(1), row),
            device_id_type=MESH,
        )

    def finish_chunk(pair, r):
        @pl.loop(0, 2)
        def _(s):
            t = 2 * pair + s
            sum_copy(t, s, r).wait_recv()
            at = pl.ds(pl.multiple_of(r * LANES, LANES), LANES)
            to = pl.ds(pl.multiple_of(r * LANES + RIM, RIM), LANES)
            fin[t, to] = part[t, 0, at] + from_sum[t, at] + from_one[t, at]

    def finish_last(pair):
        @pl.loop(0, 2)
        def _(s):
            tile_copy(2 * pair + s, s, 1).wait_recv()

        finish_chunk(pair, chunks - 1)

        @pl.loop(0, 2)
        def _(s):
            rim_copy(2 * pair + s).start()

    def finish_rim(pair):
        @pl.loop(0, 2)
        def _(s):
            rim_copy(2 * pair + s).wait_recv()

    def finish(pair):
        finish_last(pair)

        @pl.loop(1, chunks)
        def _(i):
            finish_chunk(pair, chunks - 1 - i)

        finish_rim(pair)

    def shaped(t, r):
        j, g = TILES[t]
        near = fin[t, pl.ds(pl.multiple_of(r * LANES, LANES), LANES + RIM)]
        tap = [taps_ref[i, j : j + 1, g * wide : (g + 1) * wide] for i in range(3)]
        return (
            tap[0] * near[RIM:] + tap[1] * near[RIM - 1 : RIM - 1 + LANES] + tap[2] * near[RIM - 2 : RIM - 2 + LANES]
        )

    def swap_start(which, g, source, target):
        @pl.loop(1, blocks)
        def _(i):
            p = peer(i)
            if which == 2:
                src, dst = source.at[g, p], target.at[g, pl.ds(pl.multiple_of(me * per, per), per)]
            else:
                src, dst = source.at[g, pl.ds(pl.multiple_of(p * per, per), per)], target.at[g, me]
            pltpu.make_async_remote_copy(
                src_ref=src,
                dst_ref=dst,
                send_sem=swap_send.at[which, g],
                recv_sem=swap_recv.at[which, g],
                device_id=(p, row),
                device_id_type=MESH,
            ).start()

        own = pl.ds(pl.multiple_of(me * per, per), per)
        if which == 2:
            target[g, own] = source[g, me]
        else:
            target[g, me] = source[g, own]

    def swap_wait(sem, which, g):
        held = h_got.at[0, pl.ds(0, peers)]
        pltpu.make_async_copy(held, held, sem.at[which, g]).wait()

    def times_tables(value):
        high, low = split(value)
        result = []
        for i in (0, 2):
            both = jnp.dot(jnp.concatenate([high, low], axis=0), table[i], preferred_element_type=F32)
            result.append(both[: 2 * half] + both[2 * half :] + jnp.dot(high, table[i + 1], preferred_element_type=F32))
        return result

    def spectrum(source, g):
        @pl.loop(0, chunks)
        def _(r):
            at = pl.ds(pl.multiple_of(r * LANES, LANES), LANES)
            found = real_dft([source[g, s, :, at] for s in range(blocks)])
            for k, (re, im) in enumerate(found):
                c, s = turn_ref[0, k : k + 1, at], turn_ref[1, k : k + 1, at]
                work[k * per : (k + 1) * per, at] = re * c if im is None else re * c + im * s
                work[half + k * per : half + (k + 1) * per, at] = -re * s if im is None else im * c - re * s

        by_cos, by_sin = times_tables(work[...])
        return by_cos[:half] + by_sin[half:], by_cos[half:] - by_sin[:half]

    def convolve(g):
        re, im = spectrum(u_got, g)
        h_re, h_im = h_freq[g, :half], h_freq[g, half:]
        product = jnp.concatenate([re * h_re - im * h_im, re * h_im + im * h_re], axis=0)
        by_cos, by_sin = times_tables(product)
        work[:half] = by_cos[:half] - by_sin[half:]
        work[half:] = by_cos[half:] + by_sin[:half]

        @pl.loop(0, chunks)
        def _(r):
            at = pl.ds(pl.multiple_of(r * LANES, LANES), LANES)
            freq = []
            for k in range(freqs):
                c, s = turn_ref[0, k : k + 1, at], turn_ref[1, k : k + 1, at]
                re, im = work[k * per : (k + 1) * per, at], work[half + k * per : half + (k + 1) * per, at]
                freq.append((re * c - im * s, None if k in (0, freqs - 1) else re * s + im * c))
            for s, value in enumerate(real_inverse(freq, blocks)):
                y_sent[g, s, :, at] = value

    def gate(g):
        for r in range(chunks):
            at = slice(r * LANES, (r + 1) * LANES)
            u = shaped(2 * g, r) * shaped(2 * g + 1, r)
            u_kept[g, at] = u
            u_sent[g, :, at] = u.T
        swap_start(1, g, u_sent, u_got)

    def through(g):
        swap_wait(swap_recv, 1, g)
        convolve(g)
        swap_start(2, g, y_sent, y_got)

    def sent(pair):
        @pl.loop(0, 2)
        def _(s):
            t = 2 * pair + s
            if pair > 0:
                tile_copy(t, s, 0).wait_send()
            tile_copy(t, s, 1).wait_send()
            rim_copy(t).wait_send()

            @pl.loop(0, chunks)
            def _(r):
                sum_copy(t, s, r).wait_send()

    def result(r):
        at = pl.ds(pl.multiple_of(r * LANES, LANES), LANES)
        for g in range(2):
            out_ref[at, g * wide : (g + 1) * wide] = shaped(4 + g, r) * u_kept[g, at]

    send_first()
    meet(0)
    meet(1)
    send_one(0)
    h_copy.start()
    fetch(0)
    meet(2)
    fetch(1)
    h_copy.wait()
    for g in range(2):
        for r in range(chunks):
            at = slice(r * LANES, (r + 1) * LANES)
            h_sent[g, :, at] = h_ref[at, g * wide : (g + 1) * wide].T
    meet(3)
    project_rest(0)
    meet(4)
    for copy in side_copies:
        copy.start()
    send_sum(0)
    meet(5)
    for g in range(2):
        swap_start(0, g, h_sent, h_got)
    fetch(2)
    send_far(1)
    send_one(1)
    project_rest(1)
    for copy in side_copies:
        copy.wait()
    scale = 1.0 / (blocks * rows)
    for g in range(2):
        swap_wait(swap_recv, 0, g)

    @pl.loop(0, 2)
    def _(g):
        re, im = spectrum(h_got, g)
        h_freq[g, :half] = re * scale
        h_freq[g, half:] = im * scale

    finish(0)
    gate(0)
    send_sum(1)
    send_far(2)
    send_one(2)
    project_rest(2)
    through(0)
    finish(1)
    gate(1)
    send_sum(2)
    through(1)
    for g in range(2):
        swap_wait(swap_recv, 2, g)
        for r in range(chunks):
            at = slice(r * LANES, (r + 1) * LANES)
            u_kept[g, at] = y_got[g, :, at].T + gain_ref[:, g * wide : (g + 1) * wide] * u_kept[g, at]
    @pl.loop(0, chunks)
    def _(r):
        for s in range(2):
            far_copy(s, s, r).wait_send()

    sent(0)
    sent(1)
    for which in range(3):
        for g in range(2):
            swap_wait(swap_send, which, g)
    finish_last(2)

    @pl.loop(1, chunks)
    def _(i):
        r = chunks - 1 - i
        finish_chunk(2, r)
        result(r + 1)

    finish_rim(2)
    result(0)

    sent(2)


def on_device(blocks, sequence, w_proj, short_filter, long_filter, skip_gain):
    rows, depth = sequence.shape
    channels = long_filter.shape[1]
    wide = channels // 2
    per = wide // blocks
    freqs = blocks // 2 + 1
    tiles = len(TILES)
    *turn_tables, turn_cos, turn_sin = tables(blocks, rows)
    vmem = pl.BlockSpec(memory_space=pltpu.VMEM)
    hbm = pl.BlockSpec(memory_space=pl.ANY)
    tile = (tiles, rows, wide)
    sharded = (2, blocks, per, rows)
    flipped = (2, wide, rows)
    return pl.pallas_call(
        functools.partial(kernel, blocks),
        out_shape=pltpu.VMEM((rows, channels), F32),
        in_specs=[hbm] * 7,
        out_specs=vmem,
        scratch_shapes=[
            pltpu.VMEM((rows, depth), BF16),
            pltpu.VMEM(short_filter.shape, F32),
            pltpu.VMEM((rows, channels), F32),
            pltpu.VMEM((1, channels), F32),
            pltpu.VMEM((2, freqs, rows), F32),
            pltpu.VMEM((tiles, 4, depth, wide), BF16),
            pltpu.VMEM((4, rows, rows), BF16),
            pltpu.VMEM((tiles, 4, rows, wide), F32),
            pltpu.VMEM(tile, F32),
            pltpu.VMEM(tile, F32),
            pltpu.VMEM(tile, F32),
            pltpu.VMEM((tiles, rows + RIM, wide), F32),
            pltpu.VMEM(flipped, F32),
            pltpu.VMEM(sharded, F32),
            pltpu.VMEM((2, rows, wide), F32),
            pltpu.VMEM(flipped, F32),
            pltpu.VMEM(sharded, F32),
            pltpu.VMEM(sharded, F32),
            pltpu.VMEM(flipped, F32),
            pltpu.VMEM((2, 2 * freqs * per, rows), F32),
            pltpu.VMEM((2 * freqs * per, rows), F32),
            pltpu.SemaphoreType.DMA((tiles, 4)),
            pltpu.SemaphoreType.DMA((rows // LANES,)),
            pltpu.SemaphoreType.DMA((5,)),
            pltpu.SemaphoreType.DMA((2, rows // LANES)),
            pltpu.SemaphoreType.DMA((2, rows // LANES)),
            pltpu.SemaphoreType.DMA((tiles, rows // LANES)),
            pltpu.SemaphoreType.DMA((tiles, rows // LANES)),
            pltpu.SemaphoreType.REGULAR((blocks.bit_length() - 1,)),
            pltpu.SemaphoreType.DMA((2, tiles)),
            pltpu.SemaphoreType.DMA((2, tiles)),
            pltpu.SemaphoreType.DMA((tiles,)),
            pltpu.SemaphoreType.DMA((tiles,)),
            pltpu.SemaphoreType.DMA((3, 2)),
            pltpu.SemaphoreType.DMA((3, 2)),
        ],
        compiler_params=pltpu.CompilerParams(
            collective_id=0, has_side_effects=True, vmem_limit_bytes=56 << 20
        ),
        cost_estimate=pl.CostEstimate(
            flops=2 * rows * depth * 12 * channels, bytes_accessed=16 << 20, transcendentals=0
        ),
    )(
        sequence,
        w_proj.transpose(1, 0, 2),
        short_filter,
        long_filter,
        skip_gain[None, :],
        np.stack(turn_tables),
        np.stack([turn_cos, turn_sin]),
    )


def solution(mesh):
    return jax.shard_map(
        functools.partial(on_device, mesh.shape["ctx"]),
        mesh=mesh,
        in_specs=(
            P("ctx", "col"),
            P("col", None, None),
            P(None, None, "col"),
            P("ctx", "col"),
            P("col"),
        ),
        out_specs=P("ctx", "col"),
        check_vma=False,
    )
```
